32 devices in a mesh: ctx: 8 (over y, x, core), ep: 4 (over z).
Axes of the slice: x: 2, y: 2, z: 4, core: 2. Of those that a mesh axis runs over, the one named last changes fastest.
Arguments:
- block_input_rows: bfloat16 [4096, 4096], P(('ctx', 'ep')), may hold values from -6 to 6
- output_gradient: bfloat16 [4096, 4096], P(('ctx', 'ep')), may hold values from -12 to 12
- expert_choice_index: int32 [4096, 8], P(('ctx', 'ep')), may hold values from 0 to 31, all different within a row; in each aligned block of 128 rows (0 to 127, 128 to 255, ...) at most 36 rows name the same one
- routing_weight_rows: float32 [4096, 8], P(('ctx', 'ep')), may hold values from 0.03 to 0.5
- frozen_gate_weight: bfloat16 [32, 4096, 768], P(('ctx', 'ep')), may hold values from -0.09375 to 0.09375
- frozen_up_weight: bfloat16 [32, 4096, 768], P(('ctx', 'ep')), may hold values from -0.09375 to 0.09375
- frozen_down_weight: bfloat16 [32, 768, 4096], P(('ctx', 'ep')), may hold values from -0.21875 to 0.21875
- gate_adapter_inmap: bfloat16 [32, 16, 4096], P(('ctx', 'ep')), may hold values from -0.09375 to 0.09375
- gate_adapter_outmap: bfloat16 [32, 16, 768], P(('ctx', 'ep')), may hold values from -0.21875 to 0.21875
- up_adapter_inmap: bfloat16 [32, 16, 4096], P(('ctx', 'ep')), may hold values from -0.09375 to 0.09375
- up_adapter_outmap: bfloat16 [32, 16, 768], P(('ctx', 'ep')), may hold values from -0.21875 to 0.21875
- down_adapter_inmap: bfloat16 [32, 16, 768], P(('ctx', 'ep')), may hold values from -0.21875 to 0.21875
- down_adapter_outmap: bfloat16 [32, 16, 4096], P(('ctx', 'ep')), may hold values from -0.09375 to 0.09375
- stored_gate_preact: bfloat16 [32, 1152, 768], P(('ctx', 'ep')), may hold values from -8 to 8
- stored_up_preact: bfloat16 [32, 1152, 768], P(('ctx', 'ep')), may hold values from -6 to 6
Outputs:
- grad_in: bfloat16 [4096, 4096], P(('ctx', 'ep'))
- gate_input_gradient: bfloat16 [32, 16, 4096], P(('ctx', 'ep'))
- gate_output_gradient: bfloat16 [32, 16, 768], P(('ctx', 'ep'))
- up_input_gradient: bfloat16 [32, 16, 4096], P(('ctx', 'ep'))
- up_output_gradient: bfloat16 [32, 16, 768], P(('ctx', 'ep'))
- down_input_gradient: bfloat16 [32, 16, 768], P(('ctx', 'ep'))
- down_output_gradient: bfloat16 [32, 16, 4096], P(('ctx', 'ep'))
The draws below stay inside these ranges and needn't reach their ends.
Inputs may be any that keep to these rules, and one draw needn't show every extreme that they name: `expert_choice_index`: A token names 8 different experts. Among the tokens of one device, an expert is named by at most 36 of them, and in every draw some expert by exactly 36.
All inputs are finite; a program needn't handle non-finite values.
Results may differ from the reference program's by a relative error of at most 0.0065.
Values may be sent and summed in bfloat16 or wider, within the bound.
No kernel may reach another device: no remote copies, remote signals or barrier semaphores. Data moves between devices by JAX's collectives and lax.ppermute only.
A program may use at most 256 MiB of HBM per device.

```python
import math
import jax
import jax.numpy as jnp
import numpy as np
from jax import lax

HIDDEN_WIDTH = 4096
HALF_HIDDEN = 768
ADAPTER_RANK = 16
TOPK = 8
TOK_DEV = 128
EXPERT_COUNT = 32
TOKENS = 4096
CAP = 36
SLOTS = 1152


def block_levels(stream_key, shape, cuts, low, top_value):
    factor_of, own = 1.0, jax.random.fold_in(stream_key, 6)
    for position, blocks in cuts:
        heights = jnp.exp(jax.random.uniform(jax.random.fold_in(own, position), (blocks,), jnp.float32, low / len(cuts), top_value / len(cuts)))
        factor_of = factor_of * jnp.repeat(heights, shape[position] // blocks).reshape([-1 if axis == position else 1 for axis in range(len(shape))])
    return factor_of


def deal_out(rng, own, number, rows, number_of, top, limit, skew):
    ranking = jax.random.permutation(rng, number_of)
    packed, usual = portions_of(number_of, rows * top, limit, skew, True), portions_of(number_of, rows * top, limit, skew, False)
    places = jnp.arange(number_of)

    def named(tallies, offset_by):
        used = int((tallies > 0).sum())
        fixed = max(1, used // 4)
        moved = fixed + (places - fixed + offset_by * (used - fixed)) % max(1, number_of - fixed)
        return jnp.zeros((number_of,), jnp.int32).at[ranking[jnp.where(places < fixed, places, moved)]].set(jnp.asarray(tallies, jnp.int32))

    tallies = jnp.where(number % 4 == 0, named(packed, number // 4), named(usual, number - number // 4 - 1))
    mixed = jax.random.permutation(jax.random.fold_in(own, 3), number_of)
    donor, taker = mixed[0:number_of // 2 * 2:2], mixed[1:number_of // 2 * 2:2]
    room = jnp.minimum(tallies[donor] - 1, limit - tallies[taker]) // 2
    room = jnp.where((donor == ranking[0]) | (taker == ranking[0]) | (tallies[taker] == 0), 0, jnp.maximum(room, 0))
    moved = jax.random.randint(jax.random.fold_in(own, 4), (number_of // 2,), 0, 1 << 20) % (room + 1)
    tallies = tallies.at[donor].add(-moved).at[taker].add(moved)
    items = jnp.searchsorted(jnp.cumsum(tallies), jnp.arange(rows * top), side="right").astype(jnp.int32)
    table = items.reshape(top, rows).T
    table = table[jax.random.permutation(jax.random.fold_in(own, 1), rows)]
    offset_by = jax.random.randint(jax.random.fold_in(own, 2), (rows, 1), 0, top)
    return jnp.take_along_axis(table, (jnp.arange(top)[None, :] + offset_by) % top, axis=1)


def portions_of(number_of, total, reach, lean, full):
    portions = [(1 << 20) // math.isqrt(rank ** lean) + 1 for rank in range(1, number_of + 1)]
    largest = reach if full else min(reach, max(-(-total // number_of), total * portions[0] // sum(portions)))
    least = 1 if total - largest >= number_of - 1 else 0
    given, rest = [largest] + [least] * (number_of - 1), total - largest - least * (number_of - 1)
    while rest > 0:
        candidates = [i for i in range(1, number_of) if given[i] < largest] or [i for i in range(1, number_of) if given[i] < reach]
        whole, left = sum([portions[i] for i in candidates]), rest
        for i in candidates:
            addition = min(reach - given[i], max(1, left * portions[i] // whole), rest)
            given[i] = given[i] + addition
            rest = rest - addition
    return np.array(given)


def gaussian(key, shape, width, bound, split=(), held_as=jnp.bfloat16):
    array = width * jax.random.normal(key, shape, jnp.float32)
    if split:
        array = array * block_levels(key, shape, split, -0.22, 0.18)
    return jnp.clip(array, -bound, bound).astype(held_as)


def setup_inputs(seed: int = 0) -> dict:
    key_of = jax.random.split(jax.random.key(seed), 16)
    block_input_rows = gaussian(key_of[0], (TOKENS, HIDDEN_WIDTH), 1.0, 6.0, ((0, 32),))
    output_gradient = gaussian(key_of[1], (TOKENS, HIDDEN_WIDTH), 2.0, 12.0, ((0, 32),))
    expert_choice_index_keys = jax.random.split(jax.random.fold_in(key_of[2], 1), TOKENS // TOK_DEV)
    expert_choice_index_turns = jax.random.permutation(jax.random.fold_in(key_of[2], 3), TOKENS // TOK_DEV)
    expert_choice_index = jax.vmap(lambda own, number: deal_out(jax.random.fold_in(key_of[2], 2), own, number, TOK_DEV, EXPERT_COUNT, TOPK, CAP, 2))(expert_choice_index_keys, expert_choice_index_turns).reshape((TOKENS, TOPK))
    routing_weight_rows = jnp.clip(jnp.exp(math.log(0.5) - 2.8134107 * jax.random.uniform(key_of[3], (TOKENS, TOPK), jnp.float32) ** block_levels(key_of[3], (TOKENS, TOPK), ((0, 32),), -0.2, 0.2)), 0.03, 0.5)
    frozen_gate_weight = gaussian(key_of[4], (EXPERT_COUNT, HIDDEN_WIDTH, HALF_HIDDEN), HIDDEN_WIDTH ** -0.5, 0.09375, ((0, 32),))
    frozen_up_weight = gaussian(key_of[5], (EXPERT_COUNT, HIDDEN_WIDTH, HALF_HIDDEN), HIDDEN_WIDTH ** -0.5, 0.09375, ((0, 32),))
    frozen_down_weight = gaussian(key_of[6], (EXPERT_COUNT, HALF_HIDDEN, HIDDEN_WIDTH), HALF_HIDDEN ** -0.5, 0.21875, ((0, 32),))
    gate_adapter_inmap = gaussian(key_of[7], (EXPERT_COUNT, ADAPTER_RANK, HIDDEN_WIDTH), HIDDEN_WIDTH ** -0.5, 0.09375, ((0, 32),))
    gate_adapter_outmap = gaussian(key_of[8], (EXPERT_COUNT, ADAPTER_RANK, HALF_HIDDEN), HALF_HIDDEN ** -0.5, 0.21875, ((0, 32),))
    up_adapter_inmap = gaussian(key_of[9], (EXPERT_COUNT, ADAPTER_RANK, HIDDEN_WIDTH), HIDDEN_WIDTH ** -0.5, 0.09375, ((0, 32),))
    up_adapter_outmap = gaussian(key_of[10], (EXPERT_COUNT, ADAPTER_RANK, HALF_HIDDEN), HALF_HIDDEN ** -0.5, 0.21875, ((0, 32),))
    down_adapter_inmap = gaussian(key_of[11], (EXPERT_COUNT, ADAPTER_RANK, HALF_HIDDEN), HALF_HIDDEN ** -0.5, 0.21875, ((0, 32),))
    down_adapter_outmap = gaussian(key_of[12], (EXPERT_COUNT, ADAPTER_RANK, HIDDEN_WIDTH), HIDDEN_WIDTH ** -0.5, 0.09375, ((0, 32),))
    stored_gate_preact = gaussian(key_of[13], (EXPERT_COUNT, SLOTS, HALF_HIDDEN), 1.5, 8.0, ((0, 32),))
    stored_up_preact = gaussian(key_of[14], (EXPERT_COUNT, SLOTS, HALF_HIDDEN), 1.0, 6.0, ((0, 32),))
    return dict(block_input_rows=block_input_rows, output_gradient=output_gradient, expert_choice_index=expert_choice_index, routing_weight_rows=routing_weight_rows, frozen_gate_weight=frozen_gate_weight, frozen_up_weight=frozen_up_weight, frozen_down_weight=frozen_down_weight, gate_adapter_inmap=gate_adapter_inmap, gate_adapter_outmap=gate_adapter_outmap, up_adapter_inmap=up_adapter_inmap, up_adapter_outmap=up_adapter_outmap, down_adapter_inmap=down_adapter_inmap, down_adapter_outmap=down_adapter_outmap, stored_gate_preact=stored_gate_preact, stored_up_preact=stored_up_preact)


adapter_scale = 2.0


def contract_matrices(left_mat, right_mat, left_axis, right_axis):
    return lax.dot_general(left_mat, right_mat, (((left_axis,), (right_axis,)), ((), ())), preferred_element_type=jnp.float32)


def expert_backward(gathered_input_rows, gathered_gradient_rows, gate_pre, up_pre, frozen_gate_weight, frozen_up_weight, frozen_down_weight, gate_adapter_input, gate_out, up_adapter_input, up_out, down_adapter_input, down_adapter_output):
    gate_value = gate_pre.astype(jnp.float32)
    up_value = up_pre.astype(jnp.float32)
    sigmoid_gate = jax.nn.sigmoid(gate_value)
    silu_gate = gate_value * sigmoid_gate
    hidden_activation = (silu_gate * up_value).astype(jnp.bfloat16)
    down_adapter_delta = contract_matrices(hidden_activation, down_adapter_input, 1, 1).astype(jnp.bfloat16)
    adapter_gradient = contract_matrices(gathered_gradient_rows, down_adapter_output, 1, 1).astype(jnp.bfloat16)
    down_output_gradient = adapter_scale * contract_matrices(down_adapter_delta, gathered_gradient_rows, 0, 0)
    down_input_gradient = adapter_scale * contract_matrices(adapter_gradient, hidden_activation, 0, 0)
    hidden_gradient_rows = contract_matrices(gathered_gradient_rows, frozen_down_weight, 1, 1) + adapter_scale * contract_matrices(adapter_gradient, down_adapter_input, 1, 0)
    gate_gradient_rows = (hidden_gradient_rows * up_value * sigmoid_gate * (1.0 + gate_value * (1.0 - sigmoid_gate))).astype(jnp.bfloat16)
    up_gradient_rows = (hidden_gradient_rows * silu_gate).astype(jnp.bfloat16)
    gate_adapter_delta = contract_matrices(gathered_input_rows, gate_adapter_input, 1, 1).astype(jnp.bfloat16)
    up_adapter_delta = contract_matrices(gathered_input_rows, up_adapter_input, 1, 1).astype(jnp.bfloat16)
    gate_output_gradient = adapter_scale * contract_matrices(gate_adapter_delta, gate_gradient_rows, 0, 0)
    up_output_gradient = adapter_scale * contract_matrices(up_adapter_delta, up_gradient_rows, 0, 0)
    gate_backward_rows = contract_matrices(gate_gradient_rows, gate_out, 1, 1).astype(jnp.bfloat16)
    up_backward_rows = contract_matrices(up_gradient_rows, up_out, 1, 1).astype(jnp.bfloat16)
    gate_input_gradient = adapter_scale * contract_matrices(gate_backward_rows, gathered_input_rows, 0, 0)
    up_input_gradient = adapter_scale * contract_matrices(up_backward_rows, gathered_input_rows, 0, 0)
    scattered_output_rows = contract_matrices(gate_gradient_rows, frozen_gate_weight, 1, 1) + contract_matrices(up_gradient_rows, frozen_up_weight, 1, 1)
    scattered_output_rows = scattered_output_rows + adapter_scale * (contract_matrices(gate_backward_rows, gate_adapter_input, 1, 0) + contract_matrices(up_backward_rows, up_adapter_input, 1, 0))
    expert_outcomes = (gate_input_gradient.astype(jnp.bfloat16), gate_output_gradient.astype(jnp.bfloat16), up_input_gradient.astype(jnp.bfloat16), up_output_gradient.astype(jnp.bfloat16), down_input_gradient.astype(jnp.bfloat16), down_output_gradient.astype(jnp.bfloat16))
    return scattered_output_rows.astype(jnp.bfloat16), expert_outcomes


def reference(block_input_rows, output_gradient, expert_choice_index, routing_weight_rows, frozen_gate_weight, frozen_up_weight, frozen_down_weight, gate_adapter_inmap, gate_adapter_outmap, up_adapter_inmap, up_adapter_outmap, down_adapter_inmap, down_adapter_outmap, stored_gate_preact, stored_up_preact):
    blocks = TOKENS // TOK_DEV
    pick_count = TOK_DEV * TOPK
    block_ids = expert_choice_index.reshape(blocks, pick_count)
    onehot = (block_ids[:, :, None] == jnp.arange(EXPERT_COUNT, dtype=jnp.int32)[None, None, :]).astype(jnp.int32)
    running = jnp.cumsum(onehot, axis=1, dtype=jnp.int32)
    slot_num = jnp.sum(onehot * running, axis=2).astype(jnp.int32) - 1
    slot_global = (jnp.arange(blocks, dtype=jnp.int32)[:, None] * CAP + slot_num).reshape(-1).astype(jnp.int32)
    flat_ids = expert_choice_index.reshape(-1).astype(jnp.int32)
    token_pick = (jnp.arange(TOKENS * TOPK, dtype=jnp.int32) // TOPK).astype(jnp.int32)
    token_index_table = jnp.full((EXPERT_COUNT, SLOTS), TOKENS, jnp.int32).at[flat_ids, slot_global].set(token_pick)
    routing_weight_table = jnp.zeros((EXPERT_COUNT, SLOTS), routing_weight_rows.dtype).at[flat_ids, slot_global].set(routing_weight_rows.reshape(-1))

    def single_expert_backward(carried, entries):
        (tokens_here, weights_here, gate_w, up_w, down_w, gate_adapter_input, gate_out, up_adapter_input, up_out, down_adapter_input, down_adapter_output, gate_pre, up_pre) = entries
        filled = tokens_here < TOKENS
        safe_index = jnp.minimum(tokens_here, TOKENS - 1)
        gathered_input_rows = jnp.where(filled[:, None], block_input_rows[safe_index], jnp.zeros((), block_input_rows.dtype))
        gathered_gradient_rows = (weights_here[:, None] * output_gradient[safe_index].astype(jnp.float32)).astype(jnp.bfloat16)
        scattered_output_rows, expert_outcomes = expert_backward(gathered_input_rows, gathered_gradient_rows, gate_pre, up_pre, gate_w, up_w, down_w, gate_adapter_input, gate_out, up_adapter_input, up_out, down_adapter_input, down_adapter_output)
        carried = carried.at[tokens_here].add(scattered_output_rows.astype(jnp.float32))
        return carried, expert_outcomes

    initial_sum_state = jnp.zeros((TOKENS + 1, HIDDEN_WIDTH), jnp.float32)
    reduced_total, expert_outcomes = lax.scan(single_expert_backward, initial_sum_state, (token_index_table, routing_weight_table, frozen_gate_weight, frozen_up_weight, frozen_down_weight, gate_adapter_inmap, gate_adapter_outmap, up_adapter_inmap, up_adapter_outmap, down_adapter_inmap, down_adapter_outmap, stored_gate_preact, stored_up_preact))
    grad_in = reduced_total[:TOKENS].astype(jnp.bfloat16)
    return grad_in, expert_outcomes[0], expert_outcomes[1], expert_outcomes[2], expert_outcomes[3], expert_outcomes[4], expert_outcomes[5]
```

```python
import jax
import jax.numpy as jnp
from jax import lax
from jax.sharding import PartitionSpec as P

scale = 2.0
chunks = 4


def dot(a, b, da, db):
    return lax.dot_general(
        a, b, (((da,), (db,)), ((), ())), preferred_element_type=jnp.float32
    )


def local(
    x,
    grad,
    ids,
    weights,
    gate_w,
    up_w,
    down_w,
    gate_in,
    gate_out,
    up_in,
    up_out,
    down_in,
    down_out,
    gate_pre,
    up_pre,
):
    gate_w, up_w, down_w = gate_w[0], up_w[0], down_w[0]
    gate_in, gate_out, up_in, up_out = gate_in[0], gate_out[0], up_in[0], up_out[0]
    down_in, down_out, gate_pre, up_pre = down_in[0], down_out[0], gate_pre[0], up_pre[0]
    tok, width = x.shape
    rank = gate_in.shape[0]
    nc, ne = lax.axis_size("ctx"), lax.axis_size("ep")
    slots = gate_pre.shape[0]
    rows = slots // nc
    cap = rows // ne
    me = lax.axis_index("ep")
    cols = width // chunks
    bf, f32 = jnp.bfloat16, jnp.float32

    packed = jnp.concatenate([ids.astype(f32), weights], axis=1)
    packed = lax.all_gather(packed, "ep")
    top = ids.shape[1]
    ids_all = packed[:, :, :top].astype(jnp.int32)
    w_all = packed[:, :, top:]
    mine = jnp.arange(nc, dtype=jnp.int32) * ne + me
    hit = ids_all[:, :, None, :] == mine[None, None, :, None]
    sel = jnp.any(hit, axis=3)
    wt = jnp.sum(jnp.where(hit, w_all[:, :, None, :], 0.0), axis=3)
    iota = jnp.arange(tok, dtype=jnp.int32)
    lower = (iota[:, None] > iota[None, :]).astype(bf)
    place = jnp.einsum("ts,esc->cet", lower, sel.astype(bf), preferred_element_type=f32)
    key = place.astype(jnp.int32) + (jnp.arange(ne, dtype=jnp.int32) * cap)[None, :, None]
    key = jnp.where(jnp.transpose(sel, (2, 0, 1)), key, -1).reshape(nc, 1, ne * tok)
    wt = jnp.transpose(wt, (2, 0, 1)).reshape(nc, 1, ne * tok)
    match = key == jnp.arange(rows, dtype=jnp.int32)[None, :, None]
    pick = match.astype(bf)
    slot_w = jnp.sum(jnp.where(match, wt, 0.0), axis=2, keepdims=True)

    got = []
    for q in range(chunks):
        part = lax.all_gather(grad[:, q * cols : (q + 1) * cols], "ep", tiled=True)
        sent = (dot(pick, part, 2, 0) * slot_w).astype(bf)
        got.append(
            lax.all_to_all(sent, "ctx", split_axis=0, concat_axis=0, tiled=True).reshape(slots, cols)
        )
    both_in = jnp.concatenate([gate_in, up_in], axis=0)
    both_all = lax.all_gather(both_in, "ctx", tiled=True)
    x_all = lax.all_gather(x, "ep", tiled=True)
    lora_tok = dot(x_all, both_all, 1, 1).astype(bf).reshape(ne * tok, nc, 2 * rank)
    lora_slot = jnp.einsum("cjt,tcr->cjr", pick, lora_tok, preferred_element_type=f32).astype(bf)
    lora = lax.all_to_all(lora_slot, "ctx", split_axis=0, concat_axis=0, tiled=True).reshape(
        slots, 2 * rank
    )

    gate_v, up_v = gate_pre.astype(f32), up_pre.astype(f32)
    sig = jax.nn.sigmoid(gate_v)
    silu = gate_v * sig
    hidden = (silu * up_v).astype(bf)
    down_lora = dot(hidden, down_in, 1, 1).astype(bf)
    grad_lora = sum(
        dot(got[q], down_out[:, q * cols : (q + 1) * cols], 1, 1) for q in range(chunks)
    ).astype(bf)
    grad_hidden = sum(
        dot(got[q], down_w[:, q * cols : (q + 1) * cols], 1, 1) for q in range(chunks)
    ) + scale * dot(grad_lora, down_in, 1, 0)
    down_output_gradient = jnp.concatenate(
        [(scale * dot(down_lora, got[q], 0, 0)).astype(bf) for q in range(chunks)], axis=1
    )
    down_input_gradient = (scale * dot(grad_lora, hidden, 0, 0)).astype(bf)
    grad_gate = (grad_hidden * up_v * sig * (1.0 + gate_v * (1.0 - sig))).astype(bf)
    grad_up = (grad_hidden * silu).astype(bf)
    gate_output_gradient = (scale * dot(lora[:, :rank], grad_gate, 0, 0)).astype(bf)
    up_output_gradient = (scale * dot(lora[:, rank:], grad_up, 0, 0)).astype(bf)
    gate_back = dot(grad_gate, gate_out, 1, 1).astype(bf)
    up_back = dot(grad_up, up_out, 1, 1).astype(bf)
    back = jnp.concatenate([gate_back, up_back], axis=1)
    scaled_in = (both_in.astype(f32) * scale).astype(bf)

    back_tok = lax.all_to_all(
        back.reshape(nc, rows, 2 * rank), "ctx", split_axis=0, concat_axis=0, tiled=True
    )
    spread = jnp.einsum("cjr,cjt->crt", back_tok, pick, preferred_element_type=f32).astype(bf)
    share = (scale * dot(spread.reshape(nc * 2 * rank, ne * tok), x_all, 1, 0)).astype(bf)
    share = lax.all_to_all(
        share.reshape(nc, 2 * rank, width), "ctx", split_axis=0, concat_axis=0, tiled=True
    )
    both_input_gradients = jnp.sum(share.astype(f32), axis=0).astype(bf)

    outs = []
    for q in range(chunks):
        at = slice(q * cols, (q + 1) * cols)
        rows_out = (
            dot(grad_gate, gate_w[at], 1, 1)
            + dot(grad_up, up_w[at], 1, 1)
            + dot(back, scaled_in[:, at], 1, 0)
        ).astype(bf)
        returned = lax.all_to_all(
            rows_out.reshape(nc, rows, cols), "ctx", split_axis=0, concat_axis=0, tiled=True
        ).reshape(slots, cols)
        partial = dot(pick.reshape(slots, ne * tok), returned, 0, 0).astype(bf)
        parts = lax.all_to_all(
            partial.reshape(ne, tok, cols), "ep", split_axis=0, concat_axis=0, tiled=True
        )
        outs.append(jnp.sum(parts.astype(f32), axis=0).astype(bf))
    grad_in = jnp.concatenate(outs, axis=1)
    return (
        grad_in,
        both_input_gradients[None, :rank],
        gate_output_gradient[None],
        both_input_gradients[None, rank:],
        up_output_gradient[None],
        down_input_gradient[None],
        down_output_gradient[None],
    )


def solution(mesh):
    flat, deep = P(("ctx", "ep"), None), P(("ctx", "ep"), None, None)
    return jax.shard_map(
        local,
        mesh=mesh,
        in_specs=(flat,) * 4 + (deep,) * 11,
        out_specs=(flat,) + (deep,) * 6,
        check_vma=False,
    )
```

```python
import jax
import jax.numpy as jnp
from jax import lax
from jax.sharding import PartitionSpec as P

scale = 2.0
bf, f32, i32 = jnp.bfloat16, jnp.float32, jnp.int32


def dot(a, b, da, db):
    return lax.dot_general(
        a, b, (((da,), (db,)), ((), ())), preferred_element_type=jnp.float32
    )


def swap(pieces, nc):
    got = [pieces[0]]
    for j in range(1, nc):
        got.append(lax.ppermute(pieces[j], "ctx", [(c, c ^ j) for c in range(nc)]))
    return got


def one_hot(index, size):
    return (index[..., None] == jnp.arange(size, dtype=i32)).astype(bf)


def local(
    x,
    grad,
    ids,
    weights,
    gate_w,
    up_w,
    down_w,
    gate_in,
    gate_out,
    up_in,
    up_out,
    down_in,
    down_out,
    gate_pre,
    up_pre,
):
    gate_w, up_w, down_w = gate_w[0], up_w[0], down_w[0]
    gate_in, gate_out, up_in, up_out = gate_in[0], gate_out[0], up_in[0], up_out[0]
    down_in, down_out, gate_pre, up_pre = down_in[0], down_out[0], gate_pre[0], up_pre[0]
    tok, width = x.shape
    rank = gate_in.shape[0]
    nc, ne = lax.axis_size("ctx"), lax.axis_size("ep")
    slots = gate_pre.shape[0]
    rows = slots // nc
    cap = rows // ne
    part = slots // ne
    fold = ne
    cols = width // fold
    top = ids.shape[1]
    col, me = lax.axis_index("ctx"), lax.axis_index("ep")
    near = col ^ jnp.arange(nc, dtype=i32)

    def from_next(value, step):
        return lax.ppermute(value, "ep", [((e + step) % ne, e) for e in range(ne)])

    stacked = jnp.concatenate([grad[:, h * cols : (h + 1) * cols] for h in range(fold)], axis=0)
    packed = jnp.concatenate([ids.astype(f32), weights], axis=1)
    metas, grads, xs = [packed], [stacked], [x]
    for k in range(1, ne):
        metas.append(from_next(packed, k))
    for k in range(1, ne):
        grads.append(from_next(grads[-1], 1))
    for k in range(1, ne):
        xs.append(from_next(xs[-1], 1))

    both_in = jnp.concatenate([gate_in, up_in], axis=0)
    both_all = lax.all_gather(both_in, "ctx")[near].reshape(nc * 2 * rank, width)
    scaled_in = (both_in.astype(f32) * scale).astype(bf)

    mine = near * ne + me
    iota = jnp.arange(tok, dtype=i32)
    lower = (iota[:, None] > iota[None, :]).astype(bf)
    fold_iota = jnp.arange(fold, dtype=i32) * cap
    flat = jnp.arange(part, dtype=i32)
    flat_j, flat_s = flat // cap, flat % cap
    stack_of = [one_hot(flat_j * fold * cap + h * cap + flat_s, nc * fold * cap) for h in range(fold)]
    long = jnp.arange(slots, dtype=i32)
    unstack = one_hot(
        (long // cap) % fold * part + (long // (fold * cap)) * cap + long % cap, slots
    )
    down_grad = [0.0] * fold
    down_in_grad = 0.0

    keys, picks, hiddens, backs, gates, ups, returns = [], [], [], [], [], [], []
    for k in range(ne):
        chosen = metas[k][:, :top].astype(i32)
        hit = chosen[:, :, None] == mine[None, None, :]
        sel = jnp.any(hit, axis=1)
        wt = jnp.sum(jnp.where(hit, metas[k][:, top:, None], 0.0), axis=1).T
        place = dot(lower, sel.astype(bf), 1, 0).astype(i32).T
        key = jnp.where(sel.T, place, -slots)
        keys.append(key)
        key_h = (key[:, None, :] + fold_iota[None, :, None]).reshape(nc, 1, fold * tok)
        wt_h = jnp.broadcast_to(wt[:, None, :], (nc, fold, tok)).reshape(nc, 1, fold * tok)
        match = key_h == jnp.arange(fold * cap, dtype=i32)[None, :, None]
        pick = match.astype(bf)
        picks.append(pick)
        slot_w = jnp.sum(jnp.where(match, wt_h, 0.0), axis=2, keepdims=True)
        sent = [(dot(pick[j], grads[k], 1, 0) * slot_w[j]).astype(bf) for j in range(nc)]
        got = jnp.concatenate(swap(sent, nc), axis=0)
        got = [dot(stack_of[h], got, 1, 0).astype(bf) for h in range(fold)]

        at = near[flat_j] * rows + (me + k) % ne * cap + flat_s
        order = one_hot(at, slots)
        gate_v, up_v = dot(order, gate_pre, 1, 0), dot(order, up_pre, 1, 0)
        sig = jax.nn.sigmoid(gate_v)
        silu = gate_v * sig
        hidden = (silu * up_v).astype(bf)
        down_lora = dot(hidden, down_in, 1, 1).astype(bf)
        grad_lora, grad_hidden = 0.0, 0.0
        for h in range(fold):
            span = slice(h * cols, (h + 1) * cols)
            grad_lora += dot(got[h], down_out[:, span], 1, 1)
            grad_hidden += dot(got[h], down_w[:, span], 1, 1)
            down_grad[h] += dot(down_lora, got[h], 0, 0)
        grad_lora = grad_lora.astype(bf)
        grad_hidden += scale * dot(grad_lora, down_in, 1, 0)
        down_in_grad += dot(grad_lora, hidden, 0, 0)
        grad_gate = (grad_hidden * up_v * sig * (1.0 + gate_v * (1.0 - sig))).astype(bf)
        grad_up = (grad_hidden * silu).astype(bf)
        back = jnp.concatenate(
            [dot(grad_gate, gate_out, 1, 1).astype(bf), dot(grad_up, up_out, 1, 1).astype(bf)], axis=1
        )
        gates.append(grad_gate)
        ups.append(grad_up)
        backs.append(back)
        out = []
        for h in range(fold):
            span = slice(h * cols, (h + 1) * cols)
            out.append(
                (
                    dot(grad_gate, gate_w[span], 1, 1)
                    + dot(grad_up, up_w[span], 1, 1)
                    + dot(back, scaled_in[:, span], 1, 0)
                ).astype(bf)
            )
        out = jnp.concatenate(out, axis=0)
        out = [
            dot(unstack[j * rows : (j + 1) * rows], out, 1, 0).astype(bf) for j in range(nc)
        ]
        returned = jnp.concatenate(swap(out, nc), axis=0)
        partial = dot(pick.reshape(slots, fold * tok), returned, 0, 0)
        if k:
            partial = lax.ppermute(
                partial.astype(bf), "ep", [(e, (e + k) % ne) for e in range(ne)]
            ).astype(f32)
        returns.append(partial)

    total = sum(returns)
    grad_in = jnp.concatenate(
        [total[h * tok : (h + 1) * tok].astype(bf) for h in range(fold)], axis=1
    )

    x_all = jnp.concatenate(xs, axis=0)
    key_k = jnp.stack([keys[k] + k * cap for k in range(ne)], axis=1).reshape(nc, 1, ne * tok)
    pick_k = (key_k == jnp.arange(rows, dtype=i32)[None, :, None]).astype(bf)
    lora_tok = dot(x_all, both_all, 1, 1).astype(bf)
    lora = [
        dot(pick_k[j], lora_tok[:, j * 2 * rank : (j + 1) * 2 * rank], 1, 0).astype(bf)
        for j in range(nc)
    ]
    lora = jnp.concatenate(swap(lora, nc), axis=0).reshape(nc, ne, cap, 2 * rank)
    lora = jnp.transpose(lora, (1, 0, 2, 3)).reshape(slots, 2 * rank)
    gate_all, up_all = jnp.concatenate(gates, axis=0), jnp.concatenate(ups, axis=0)
    gate_output_gradient = (scale * dot(lora[:, :rank], gate_all, 0, 0)).astype(bf)
    up_output_gradient = (scale * dot(lora[:, rank:], up_all, 0, 0)).astype(bf)

    back = jnp.concatenate(backs, axis=0).reshape(ne, nc, cap, 2 * rank)
    back = jnp.transpose(back, (1, 0, 2, 3)).reshape(nc, rows, 2 * rank)
    back = swap([back[j] for j in range(nc)], nc)
    share = [
        scale * dot(dot(back[j], pick_k[j], 0, 0).astype(bf), x_all, 1, 0) for j in range(nc)
    ]
    share = [share[0]] + swap([s.astype(bf) for s in share], nc)[1:]
    both_input_gradients = sum(s.astype(f32) for s in share).astype(bf)
    down_output_gradient = jnp.concatenate([(scale * d).astype(bf) for d in down_grad], axis=1)
    return (
        grad_in,
        both_input_gradients[None, :rank],
        gate_output_gradient[None],
        both_input_gradients[None, rank:],
        up_output_gradient[None],
        (scale * down_in_grad).astype(bf)[None],
        down_output_gradient[None],
    )


def solution(mesh):
    flat, deep = P(("ctx", "ep"), None), P(("ctx", "ep"), None, None)
    return jax.shard_map(
        local,
        mesh=mesh,
        in_specs=(flat,) * 4 + (deep,) * 11,
        out_specs=(flat,) + (deep,) * 6,
        check_vma=False,
    )
```

```python
import jax
import jax.numpy as jnp
from jax import lax
from jax.sharding import PartitionSpec as P

scale = 2.0
bf, f32, i32 = jnp.bfloat16, jnp.float32, jnp.int32


def dot(a, b, da, db):
    return lax.dot_general(
        a, b, (((da,), (db,)), ((), ())), preferred_element_type=jnp.float32
    )


def swap(value, col):
    nc = value.shape[0]
    near = col ^ jnp.arange(nc, dtype=i32)
    out = value[near]
    got = [out[0]]
    for j in range(1, nc):
        got.append(lax.ppermute(out[j], "ctx", [(c, c ^ j) for c in range(nc)]))
    return jnp.stack(got)[near]


def one_hot(index, size):
    return (index[..., None] == jnp.arange(size, dtype=i32)).astype(bf)


def local(
    x,
    grad,
    ids,
    weights,
    gate_w,
    up_w,
    down_w,
    gate_in,
    gate_out,
    up_in,
    up_out,
    down_in,
    down_out,
    gate_pre,
    up_pre,
):
    gate_w, up_w, down_w = gate_w[0], up_w[0], down_w[0]
    gate_in, gate_out, up_in, up_out = gate_in[0], gate_out[0], up_in[0], up_out[0]
    down_in, down_out, gate_pre, up_pre = down_in[0], down_out[0], gate_pre[0], up_pre[0]
    tok, width = x.shape
    rank = gate_in.shape[0]
    nc, ne = lax.axis_size("ctx"), lax.axis_size("ep")
    slots = gate_pre.shape[0]
    rows = slots // nc
    cap = rows // ne
    part = slots // ne
    fold = ne
    cols = width // fold
    top = ids.shape[1]
    col, me = lax.axis_index("ctx"), lax.axis_index("ep")

    def from_next(value, step):
        return lax.ppermute(value, "ep", [((e + step) % ne, e) for e in range(ne)])

    stacked = jnp.concatenate([grad[:, h * cols : (h + 1) * cols] for h in range(fold)], axis=0)
    packed = jnp.concatenate([ids.astype(f32), weights], axis=1)
    metas = [packed] + [from_next(packed, k) for k in range(1, ne)]
    mine = jnp.arange(nc, dtype=i32) * ne + me
    iota = jnp.arange(tok, dtype=i32)
    lower = (iota[:, None] > iota[None, :]).astype(bf)
    fold_iota = jnp.arange(fold, dtype=i32) * cap

    def build(k, block):
        chosen = metas[k][:, :top].astype(i32)
        hit = chosen[:, :, None] == mine[None, None, :]
        sel = jnp.any(hit, axis=1)
        wt = jnp.sum(jnp.where(hit, metas[k][:, top:, None], 0.0), axis=1).T
        place = dot(lower, sel.astype(bf), 1, 0).astype(i32).T
        key = jnp.where(sel.T, place, -slots)
        key_h = (key[:, None, :] + fold_iota[None, :, None]).reshape(nc, 1, fold * tok)
        wt_h = jnp.broadcast_to(wt[:, None, :], (nc, fold, tok)).reshape(nc, 1, fold * tok)
        match = key_h == jnp.arange(rows, dtype=i32)[None, :, None]
        pick = match.astype(bf)
        slot_w = jnp.sum(jnp.where(match, wt_h, 0.0), axis=2, keepdims=True)
        return key, pick, (dot(pick, block, 2, 0) * slot_w).astype(bf)

    def exchange(value):
        return lax.all_to_all(value, "ctx", split_axis=0, concat_axis=0, tiled=True)

    keys, picks, gots, blocks = [], [], [], [stacked]
    for k in range(ne):
        if k:
            blocks.append(from_next(blocks[-1], 1))
        key, pick, sent = build(k, blocks[k])
        if k:
            sent, gots[-1] = lax.optimization_barrier((sent, gots[-1]))
        keys.append(key)
        picks.append(pick)
        gots.append(exchange(sent))
        if k == 0:
            first = sent
    flat = jnp.arange(part, dtype=i32)
    long = jnp.arange(slots, dtype=i32)
    flat, long, gate_pre, up_pre, first = lax.optimization_barrier(
        (flat, long, gate_pre, up_pre, first)
    )
    both_in = jnp.concatenate([gate_in, up_in], axis=0)
    both_all = lax.all_gather(both_in, "ctx", tiled=True)
    scaled_in = (both_in.astype(f32) * scale).astype(bf)
    late_x, _ = lax.optimization_barrier((x, blocks[-1]))
    xs = [x] + [from_next(late_x, k) for k in range(1, ne)]

    flat_j, flat_s = flat // cap, flat % cap
    stack_of = [one_hot(flat_j * rows + h * cap + flat_s, slots) for h in range(fold)]
    unstack = one_hot((long // cap) % fold * part + (long // rows) * cap + long % cap, slots)
    down_grad = [0.0] * fold
    down_in_grad = 0.0
    backs, gates, ups, outs = [], [], [], []
    for k in range(ne):
        order = one_hot(flat_j * rows + (me + k) % ne * cap + flat_s, slots)
        gate_v, up_v = dot(order, gate_pre, 1, 0), dot(order, up_pre, 1, 0)
        sig = jax.nn.sigmoid(gate_v)
        silu = gate_v * sig
        hidden = (silu * up_v).astype(bf)
        down_lora = dot(hidden, down_in, 1, 1).astype(bf)
        pieces = gots[k].reshape(slots, cols)
        got = [dot(stack_of[h], pieces, 1, 0).astype(bf) for h in range(fold)]
        grad_lora, grad_hidden = 0.0, 0.0
        for h in range(fold):
            span = slice(h * cols, (h + 1) * cols)
            grad_lora += dot(got[h], down_out[:, span], 1, 1)
            grad_hidden += dot(got[h], down_w[:, span], 1, 1)
            down_grad[h] += dot(down_lora, got[h], 0, 0)
        grad_lora = grad_lora.astype(bf)
        grad_hidden += scale * dot(grad_lora, down_in, 1, 0)
        down_in_grad += dot(grad_lora, hidden, 0, 0)
        grad_gate = (grad_hidden * up_v * sig * (1.0 + gate_v * (1.0 - sig))).astype(bf)
        grad_up = (grad_hidden * silu).astype(bf)
        back = jnp.concatenate(
            [dot(grad_gate, gate_out, 1, 1).astype(bf), dot(grad_up, up_out, 1, 1).astype(bf)], axis=1
        )
        gates.append(grad_gate)
        ups.append(grad_up)
        backs.append(back)
        out = []
        for h in range(fold):
            span = slice(h * cols, (h + 1) * cols)
            out.append(
                (
                    dot(grad_gate, gate_w[span], 1, 1)
                    + dot(grad_up, up_w[span], 1, 1)
                    + dot(back, scaled_in[:, span], 1, 0)
                ).astype(bf)
            )
        out = jnp.concatenate(out, axis=0)
        outs.append(dot(unstack, out, 1, 0).astype(bf).reshape(nc, rows, cols))

    total, before = 0.0, gots[-1]
    for k in list(range(1, ne)) + [0]:
        out, _ = lax.optimization_barrier((outs[k], before))
        before = exchange(out)
        partial = dot(picks[k].reshape(slots, fold * tok), before.reshape(slots, cols), 0, 0)
        if k:
            partial = lax.ppermute(
                partial.astype(bf), "ep", [(e, (e + k) % ne) for e in range(ne)]
            ).astype(f32)
        total = total + partial
    grad_in = jnp.concatenate(
        [total[h * tok : (h + 1) * tok].astype(bf) for h in range(fold)], axis=1
    )

    x_all = jnp.concatenate(xs, axis=0)
    key_k = jnp.stack([keys[k] + k * cap for k in range(ne)], axis=1).reshape(nc, 1, ne * tok)
    pick_k = (key_k == jnp.arange(rows, dtype=i32)[None, :, None]).astype(bf)
    lora_tok = dot(x_all, both_all, 1, 1).astype(bf).reshape(ne * tok, nc, 2 * rank)
    lora = jnp.einsum("jrt,tji->jri", pick_k, lora_tok, preferred_element_type=f32).astype(bf)
    lora = swap(lora, col).reshape(nc, ne, cap, 2 * rank)
    lora = jnp.transpose(lora, (1, 0, 2, 3)).reshape(slots, 2 * rank)
    gate_all, up_all = jnp.concatenate(gates, axis=0), jnp.concatenate(ups, axis=0)
    gate_output_gradient = (scale * dot(lora[:, :rank], gate_all, 0, 0)).astype(bf)
    up_output_gradient = (scale * dot(lora[:, rank:], up_all, 0, 0)).astype(bf)

    back = jnp.concatenate(backs, axis=0).reshape(ne, nc, cap, 2 * rank)
    back = swap(jnp.transpose(back, (1, 0, 2, 3)).reshape(nc, rows, 2 * rank), col)
    spread = jnp.einsum("jri,jrt->jit", back, pick_k, preferred_element_type=f32).astype(bf)
    share = scale * dot(spread.reshape(nc * 2 * rank, ne * tok), x_all, 1, 0)
    both_input_gradients = lax.psum_scatter(share, "ctx", scatter_dimension=0, tiled=True).astype(bf)
    down_output_gradient = jnp.concatenate([(scale * d).astype(bf) for d in down_grad], axis=1)
    return (
        grad_in,
        both_input_gradients[None, :rank],
        gate_output_gradient[None],
        both_input_gradients[None, rank:],
        up_output_gradient[None],
        (scale * down_in_grad).astype(bf)[None],
        down_output_gradient[None],
    )


def solution(mesh):
    flat, deep = P(("ctx", "ep"), None), P(("ctx", "ep"), None, None)
    return jax.shard_map(
        local,
        mesh=mesh,
        in_specs=(flat,) * 4 + (deep,) * 11,
        out_specs=(flat,) + (deep,) * 6,
        check_vma=False,
    )
```

```python
import jax
import jax.numpy as jnp
from jax import lax
from jax.sharding import PartitionSpec as P

scale = 2.0
dispatch_shares = (2, 3, 5, 6)
return_shares = (4, 5, 4, 3)
bf, f32, i32 = jnp.bfloat16, jnp.float32, jnp.int32


def dot(a, b, da, db):
    return lax.dot_general(
        a, b, (((da,), (db,)), ((), ())), preferred_element_type=jnp.float32
    )


def swap(value, col):
    nc = value.shape[0]
    near = col ^ jnp.arange(nc, dtype=i32)
    out = value[near]
    got = [out[0]]
    for j in range(1, nc):
        got.append(lax.ppermute(out[j], "ctx", [(c, c ^ j) for c in range(nc)]))
    return jnp.stack(got)[near]


def spans(width, shares):
    unit, at = width // sum(shares), 0
    for share in shares:
        yield slice(at * unit, (at + share) * unit)
        at += share


def local(
    x,
    grad,
    ids,
    weights,
    gate_w,
    up_w,
    down_w,
    gate_in,
    gate_out,
    up_in,
    up_out,
    down_in,
    down_out,
    gate_pre,
    up_pre,
):
    gate_w, up_w, down_w = gate_w[0], up_w[0], down_w[0]
    gate_in, gate_out, up_in, up_out = gate_in[0], gate_out[0], up_in[0], up_out[0]
    down_in, down_out, gate_pre, up_pre = down_in[0], down_out[0], gate_pre[0], up_pre[0]
    tok, width = x.shape
    rank = gate_in.shape[0]
    nc, ne = lax.axis_size("ctx"), lax.axis_size("ep")
    slots = gate_pre.shape[0]
    rows = slots // nc
    cap = rows // ne
    top = ids.shape[1]
    col, me = lax.axis_index("ctx"), lax.axis_index("ep")

    def hop(value, step):
        return lax.ppermute(value, "ep", [((e + step) % ne, e) for e in range(ne)])

    def exchange(value):
        return lax.all_to_all(value, "ctx", split_axis=0, concat_axis=0, tiled=True)

    packed = jnp.concatenate([ids.astype(f32), weights], axis=1)
    metas = [packed] + [hop(packed, k) for k in range(1, ne)]
    blocks, after = [], None
    for span in spans(width, dispatch_shares):
        own = grad[:, span]
        if after is not None:
            own, _ = lax.optimization_barrier((own, after))
        blocks.append([own] + [hop(own, k) for k in range(1, ne)])
        after = own

    metas = jnp.stack(metas)
    mine = jnp.arange(nc, dtype=i32) * ne + me
    chosen = metas[:, :, :top].astype(i32)
    hit = chosen[:, :, None, :] == mine[None, None, :, None]
    sel = jnp.any(hit, axis=3)
    wt = jnp.sum(jnp.where(hit, metas[:, :, None, top:], 0.0), axis=3)
    iota = jnp.arange(tok, dtype=i32)
    lower = (iota[:, None] > iota[None, :]).astype(bf)
    place = jnp.einsum("ts,esc->cet", lower, sel.astype(bf), preferred_element_type=f32)
    block_of = (me + jnp.arange(ne, dtype=i32)) % ne
    key = place.astype(i32) + (block_of * cap)[None, :, None]
    key = jnp.where(jnp.transpose(sel, (2, 0, 1)), key, -1).reshape(nc, 1, ne * tok)
    wt = jnp.transpose(wt, (2, 0, 1)).reshape(nc, 1, ne * tok)
    match = key == jnp.arange(rows, dtype=i32)[None, :, None]
    pick = match.astype(bf)
    slot_w = jnp.sum(jnp.where(match, wt, 0.0), axis=2, keepdims=True)

    got = []
    for parts in blocks:
        sent = (dot(pick, jnp.concatenate(parts, axis=0), 2, 0) * slot_w).astype(bf)
        if got:
            sent, got[-1] = lax.optimization_barrier((sent, got[-1]))
        got.append(exchange(sent))
    got = [g.reshape(slots, -1) for g in got]
    both_in = jnp.concatenate([gate_in, up_in], axis=0)
    late_x, late_in, _ = lax.optimization_barrier((x, both_in, tuple(blocks[-1])))
    x_all = lax.all_gather(late_x, "ep", tiled=True)
    both_all = lax.all_gather(late_in, "ctx", tiled=True)

    gate_v, up_v = gate_pre.astype(f32), up_pre.astype(f32)
    sig = jax.nn.sigmoid(gate_v)
    silu = gate_v * sig
    hidden = (silu * up_v).astype(bf)
    down_lora = dot(hidden, down_in, 1, 1).astype(bf)
    grad_lora, grad_hidden, down_grad = 0.0, 0.0, []
    for g, span in zip(got, spans(width, dispatch_shares)):
        grad_lora += dot(g, down_out[:, span], 1, 1)
        grad_hidden += dot(g, down_w[:, span], 1, 1)
        down_grad.append((scale * dot(down_lora, g, 0, 0)).astype(bf))
    grad_lora = grad_lora.astype(bf)
    grad_hidden += scale * dot(grad_lora, down_in, 1, 0)
    grad_gate = (grad_hidden * up_v * sig * (1.0 + gate_v * (1.0 - sig))).astype(bf)
    grad_up = (grad_hidden * silu).astype(bf)
    gate_back = dot(grad_gate, gate_out, 1, 1).astype(bf)
    up_back = dot(grad_up, up_out, 1, 1).astype(bf)
    back = jnp.concatenate([gate_back, up_back], axis=1)
    scaled_in = (both_in.astype(f32) * scale).astype(bf)

    grad_in, before = [], None
    for span in spans(width, return_shares):
        rows_out = (
            dot(grad_gate, gate_w[span], 1, 1)
            + dot(grad_up, up_w[span], 1, 1)
            + dot(back, scaled_in[:, span], 1, 0)
        ).astype(bf)
        if before is not None:
            rows_out, _ = lax.optimization_barrier((rows_out, before))
        before = exchange(rows_out.reshape(nc, rows, -1))
        returned = before.reshape(slots, -1)
        total = 0.0
        for k in list(range(1, ne)) + [0]:
            piece = pick[:, :, k * tok : (k + 1) * tok].reshape(slots, tok)
            partial = dot(piece, returned, 0, 0)
            total += hop(partial.astype(bf), ne - k).astype(f32) if k else partial
        grad_in.append(total.astype(bf))
    grad_in = jnp.concatenate(grad_in, axis=1)

    lora_tok = dot(x_all, both_all, 1, 1).astype(bf).reshape(ne, tok, nc, 2 * rank)
    lora_tok = lora_tok[block_of].reshape(ne * tok, nc, 2 * rank)
    lora = jnp.einsum("jrt,tji->jri", pick, lora_tok, preferred_element_type=f32).astype(bf)
    lora = swap(lora, col).reshape(slots, 2 * rank)
    gate_output_gradient = (scale * dot(lora[:, :rank], grad_gate, 0, 0)).astype(bf)
    up_output_gradient = (scale * dot(lora[:, rank:], grad_up, 0, 0)).astype(bf)

    back = swap(back.reshape(nc, rows, 2 * rank), col)
    spread = jnp.einsum("jri,jrt->jit", back, pick, preferred_element_type=f32).astype(bf)
    spread = spread.reshape(nc * 2 * rank, ne, tok)[:, (jnp.arange(ne, dtype=i32) - me) % ne]
    share = scale * dot(spread.reshape(nc * 2 * rank, ne * tok), x_all, 1, 0)
    both_input_gradients = lax.psum_scatter(share, "ctx", scatter_dimension=0, tiled=True).astype(bf)
    return (
        grad_in,
        both_input_gradients[None, :rank],
        gate_output_gradient[None],
        both_input_gradients[None, rank:],
        up_output_gradient[None],
        (scale * dot(grad_lora, hidden, 0, 0)).astype(bf)[None],
        jnp.concatenate(down_grad, axis=1)[None],
    )


def solution(mesh):
    flat, deep = P(("ctx", "ep"), None), P(("ctx", "ep"), None, None)
    return jax.shard_map(
        local,
        mesh=mesh,
        in_specs=(flat,) * 4 + (deep,) * 11,
        out_specs=(flat,) + (deep,) * 6,
        check_vma=False,
    )
```

```python
import jax
import jax.numpy as jnp
from jax import lax
from jax.sharding import PartitionSpec as P

scale = 2.0
dispatch_shares = (2, 4, 5, 5)
return_shares = (3, 5, 5, 3)
bf, f32, i32 = jnp.bfloat16, jnp.float32, jnp.int32


def dot(a, b, da, db):
    return lax.dot_general(
        a, b, (((da,), (db,)), ((), ())), preferred_element_type=jnp.float32
    )


def spread_sum(value, col):
    nc = value.shape[0]
    half = value.reshape(nc // 2, 2, *value.shape[1:])
    keep = lax.dynamic_index_in_dim(half, col % 2, 1, keepdims=False)
    give = lax.dynamic_index_in_dim(half, 1 - col % 2, 1, keepdims=False).astype(bf)
    keep = keep + lax.ppermute(give, "ctx", [(c, c ^ 1) for c in range(nc)]).astype(f32)
    total = lax.dynamic_index_in_dim(keep, col // 2, 0, keepdims=False)
    for j in range(1, nc // 2):
        out = lax.dynamic_index_in_dim(keep, col // 2 ^ j, 0, keepdims=False).astype(bf)
        total += lax.ppermute(out, "ctx", [(c, c ^ 2 * j) for c in range(nc)]).astype(f32)
    return total.astype(bf)


def spans(width, shares):
    unit, at = width // sum(shares), 0
    for share in shares:
        yield slice(at * unit, (at + share) * unit)
        at += share


def local(
    x,
    grad,
    ids,
    weights,
    gate_w,
    up_w,
    down_w,
    gate_in,
    gate_out,
    up_in,
    up_out,
    down_in,
    down_out,
    gate_pre,
    up_pre,
):
    gate_w, up_w, down_w = gate_w[0], up_w[0], down_w[0]
    gate_in, gate_out, up_in, up_out = gate_in[0], gate_out[0], up_in[0], up_out[0]
    down_in, down_out, gate_pre, up_pre = down_in[0], down_out[0], gate_pre[0], up_pre[0]
    tok, width = x.shape
    rank = gate_in.shape[0]
    nc, ne = lax.axis_size("ctx"), lax.axis_size("ep")
    slots = gate_pre.shape[0]
    rows = slots // nc
    cap = rows // ne
    top = ids.shape[1]
    col, me = lax.axis_index("ctx"), lax.axis_index("ep")

    def hop(value, step):
        return lax.ppermute(value, "ep", [((e + step) % ne, e) for e in range(ne)])

    def exchange(value):
        return lax.all_to_all(value, "ctx", split_axis=0, concat_axis=0, tiled=True)

    packed = jnp.concatenate([ids.astype(f32), weights], axis=1)
    metas = lax.all_gather(packed, "ep")
    mine = jnp.arange(nc, dtype=i32) * ne + me
    chosen = metas[:, :, :top].astype(i32)
    hit = chosen[:, :, None, :] == mine[None, None, :, None]
    sel = jnp.any(hit, axis=3)
    wt = jnp.sum(jnp.where(hit, metas[:, :, None, top:], 0.0), axis=3)
    iota = jnp.arange(tok, dtype=i32)
    lower = (iota[:, None] > iota[None, :]).astype(bf)
    place = jnp.einsum("ts,esc->cet", lower, sel.astype(bf), preferred_element_type=f32)
    key = place.astype(i32) + (jnp.arange(ne, dtype=i32) * cap)[None, :, None]
    key = jnp.where(jnp.transpose(sel, (2, 0, 1)), key, -1).reshape(nc, 1, ne * tok)
    wt = jnp.transpose(wt, (2, 0, 1)).reshape(nc, 1, ne * tok)
    match = key == jnp.arange(rows, dtype=i32)[None, :, None]
    pick = match.astype(bf)
    slot_w = jnp.sum(jnp.where(match, wt, 0.0), axis=2, keepdims=True)

    got = []
    for span in spans(width, dispatch_shares):
        block = lax.all_gather(grad[:, span], "ep", tiled=True)
        sent = (dot(pick, block, 2, 0) * slot_w).astype(bf)
        if got:
            sent, got[-1] = lax.optimization_barrier((sent, got[-1]))
        else:
            first = sent
        got.append(exchange(sent))
    got = [g.reshape(slots, -1) for g in got]

    both_in, gate_pre, up_pre, late_gate, late_up, _ = lax.optimization_barrier(
        (jnp.concatenate([gate_in, up_in], axis=0), gate_pre, up_pre, gate_w, up_w, first)
    )
    scaled_in = (both_in.astype(f32) * scale).astype(bf)
    joined = jnp.concatenate([late_gate, late_up, scaled_in.T], axis=1)
    late_x, late_in, _ = lax.optimization_barrier((x, both_in, block))
    xs = [x] + [hop(late_x, k) for k in range(1, ne)]
    both_all = lax.all_gather(late_in, "ctx", tiled=True)

    gate_v, up_v = gate_pre.astype(f32), up_pre.astype(f32)
    sig = jax.nn.sigmoid(gate_v)
    silu = gate_v * sig
    hidden = (silu * up_v).astype(bf)
    down_lora = dot(hidden, down_in, 1, 1).astype(bf)
    grad_lora, grad_hidden, down_grad = 0.0, 0.0, []
    for g, span in zip(got, spans(width, dispatch_shares)):
        grad_lora += dot(g, down_out[:, span], 1, 1)
        grad_hidden += dot(g, down_w[:, span], 1, 1)
        down_grad.append((scale * dot(down_lora, g, 0, 0)).astype(bf))
    grad_lora = grad_lora.astype(bf)
    grad_hidden += scale * dot(grad_lora, down_in, 1, 0)
    grad_gate = (grad_hidden * up_v * sig * (1.0 + gate_v * (1.0 - sig))).astype(bf)
    grad_up = (grad_hidden * silu).astype(bf)
    gate_back = dot(grad_gate, gate_out, 1, 1).astype(bf)
    up_back = dot(grad_up, up_out, 1, 1).astype(bf)
    back = jnp.concatenate([gate_back, up_back], axis=1)
    left = jnp.concatenate([grad_gate, grad_up, back], axis=1)

    grad_in, before, lora, spread = [], None, None, None
    spare = jnp.zeros((slots, 128 - 2 * rank), bf)
    for at, span in enumerate(spans(width, return_shares)):
        rows_out = dot(left, joined[span], 1, 1).astype(bf)
        ride = {0: back, 2: lora}.get(at)
        if ride is not None:
            rows_out = jnp.concatenate([rows_out, ride, spare], axis=1)
        if before is not None:
            rows_out, _ = lax.optimization_barrier((rows_out, before))
        before = exchange(rows_out.reshape(nc, rows, -1))
        wide = span.stop - span.start
        returned = before[:, :, :wide].reshape(slots, wide)
        partial = dot(pick.reshape(slots, ne * tok), returned, 0, 0).astype(bf)
        grad_in.append(lax.psum_scatter(partial, "ep", scatter_dimension=0, tiled=True))
        if at == 0:
            back_tok = before[:, :, wide : wide + 2 * rank]
            xs, _ = lax.optimization_barrier((xs, before))
            x_all = jnp.concatenate(xs, axis=0)
            block_of = (me + jnp.arange(ne, dtype=i32)) % ne
            lora_tok = dot(x_all, both_all, 1, 1).astype(bf).reshape(ne, tok, nc * 2 * rank)
            lora_tok = lora_tok[(jnp.arange(ne, dtype=i32) - me) % ne].reshape(ne * tok, nc, 2 * rank)
            lora = jnp.einsum("jrt,tji->jri", pick, lora_tok, preferred_element_type=f32)
            lora = lora.astype(bf).reshape(slots, 2 * rank)
            spread = jnp.einsum("jri,jrt->jit", back_tok, pick, preferred_element_type=f32).astype(bf)
            spread = spread.reshape(nc * 2 * rank, ne, tok)[:, block_of]
            share = scale * dot(spread.reshape(nc * 2 * rank, ne * tok), x_all, 1, 0)
            both_input_gradients = spread_sum(share.reshape(nc, 2 * rank, width), col)
        if at == 2:
            lora = before[:, :, wide : wide + 2 * rank].reshape(slots, 2 * rank)
            gate_output_gradient = (scale * dot(lora[:, :rank], grad_gate, 0, 0)).astype(bf)
            up_output_gradient = (scale * dot(lora[:, rank:], grad_up, 0, 0)).astype(bf)
    grad_in = jnp.concatenate(grad_in, axis=1)
    return (
        grad_in,
        both_input_gradients[None, :rank],
        gate_output_gradient[None],
        both_input_gradients[None, rank:],
        up_output_gradient[None],
        (scale * dot(grad_lora, hidden, 0, 0)).astype(bf)[None],
        jnp.concatenate(down_grad, axis=1)[None],
    )


def solution(mesh):
    flat, deep = P(("ctx", "ep"), None), P(("ctx", "ep"), None, None)
    return jax.shard_map(
        local,
        mesh=mesh,
        in_specs=(flat,) * 4 + (deep,) * 11,
        out_specs=(flat,) + (deep,) * 6,
        check_vma=False,
    )
```

```python
import jax
import jax.numpy as jnp
from jax import lax
from jax.sharding import PartitionSpec as P

scale = 2.0
dispatch_shares = (1, 1, 1, 1)
return_shares = (4, 5, 4, 3)
bf, f32, i32 = jnp.bfloat16, jnp.float32, jnp.int32


def dot(a, b, da, db):
    return lax.dot_general(
        a, b, (((da,), (db,)), ((), ())), preferred_element_type=jnp.float32
    )


def spread_sum(value, col):
    nc = value.shape[0]
    half = value.reshape(nc // 2, 2, *value.shape[1:])
    keep = lax.dynamic_index_in_dim(half, col % 2, 1, keepdims=False)
    give = lax.dynamic_index_in_dim(half, 1 - col % 2, 1, keepdims=False).astype(bf)
    keep = keep + lax.ppermute(give, "ctx", [(c, c ^ 1) for c in range(nc)]).astype(f32)
    total = lax.dynamic_index_in_dim(keep, col // 2, 0, keepdims=False)
    for j in range(1, nc // 2):
        out = lax.dynamic_index_in_dim(keep, col // 2 ^ j, 0, keepdims=False).astype(bf)
        total += lax.ppermute(out, "ctx", [(c, c ^ 2 * j) for c in range(nc)]).astype(f32)
    return total.astype(bf)


def spans(width, shares):
    unit, at = width // sum(shares), 0
    for share in shares:
        yield slice(at * unit, (at + share) * unit)
        at += share


def local(
    x,
    grad,
    ids,
    weights,
    gate_w,
    up_w,
    down_w,
    gate_in,
    gate_out,
    up_in,
    up_out,
    down_in,
    down_out,
    gate_pre,
    up_pre,
):
    gate_w, up_w, down_w = gate_w[0], up_w[0], down_w[0]
    gate_in, gate_out, up_in, up_out = gate_in[0], gate_out[0], up_in[0], up_out[0]
    down_in, down_out, gate_pre, up_pre = down_in[0], down_out[0], gate_pre[0], up_pre[0]
    tok, width = x.shape
    rank = gate_in.shape[0]
    nc, ne = lax.axis_size("ctx"), lax.axis_size("ep")
    slots = gate_pre.shape[0]
    rows = slots // nc
    cap = rows // ne
    top = ids.shape[1]
    col, me = lax.axis_index("ctx"), lax.axis_index("ep")

    def hop(value, step):
        return lax.ppermute(value, "ep", [((e + step) % ne, e) for e in range(ne)])

    def exchange(value):
        return lax.all_to_all(value, "ctx", split_axis=0, concat_axis=0, tiled=True)

    packed = jnp.concatenate([ids.astype(f32), weights], axis=1)
    metas = lax.all_gather(packed, "ep")
    mine = jnp.arange(nc, dtype=i32) * ne + me
    chosen = metas[:, :, :top].astype(i32)
    hit = chosen[:, :, None, :] == mine[None, None, :, None]
    sel = jnp.any(hit, axis=3)
    wt = jnp.sum(jnp.where(hit, metas[:, :, None, top:], 0.0), axis=3)
    iota = jnp.arange(tok, dtype=i32)
    lower = (iota[:, None] > iota[None, :]).astype(bf)
    place = jnp.einsum("ts,esc->cet", lower, sel.astype(bf), preferred_element_type=f32)
    key = place.astype(i32) + (jnp.arange(ne, dtype=i32) * cap)[None, :, None]
    key = jnp.where(jnp.transpose(sel, (2, 0, 1)), key, -1).reshape(nc, 1, ne * tok)
    wt = jnp.transpose(wt, (2, 0, 1)).reshape(nc, 1, ne * tok)
    match = key == jnp.arange(rows, dtype=i32)[None, :, None]
    pick = match.astype(bf)
    slot_w = jnp.sum(jnp.where(match, wt, 0.0), axis=2, keepdims=True)

    got = []
    for span in spans(width, dispatch_shares):
        block = lax.all_gather(grad[:, span], "ep", tiled=True)
        sent = (dot(pick, block, 2, 0) * slot_w).astype(bf)
        if got:
            sent, got[-1] = lax.optimization_barrier((sent, got[-1]))
        else:
            first = sent
        got.append(exchange(sent))
    got = [g.reshape(slots, -1) for g in got]

    both_in, gate_pre, up_pre, late_gate, late_up, _ = lax.optimization_barrier(
        (jnp.concatenate([gate_in, up_in], axis=0), gate_pre, up_pre, gate_w, up_w, first)
    )
    scaled_in = (both_in.astype(f32) * scale).astype(bf)
    joined = jnp.concatenate([late_gate, late_up, scaled_in.T], axis=1)
    inner = 2 * gate_w.shape[1]
    choose = (
        jnp.arange(128, dtype=i32)[:, None] + inner == jnp.arange(inner + 2 * rank, dtype=i32)[None, :]
    ).astype(bf)
    late_x, _ = lax.optimization_barrier((x, block))
    xs = [x] + [hop(late_x, k) for k in range(1, ne)]
    late_in, got[-1] = lax.optimization_barrier((both_in, got[-1]))
    both_all = lax.all_gather(late_in, "ctx", tiled=True)

    gate_v, up_v = gate_pre.astype(f32), up_pre.astype(f32)
    sig = jax.nn.sigmoid(gate_v)
    silu = gate_v * sig
    hidden = (silu * up_v).astype(bf)
    down_lora = dot(hidden, down_in, 1, 1).astype(bf)
    grad_lora, grad_hidden, down_grad = 0.0, 0.0, []
    for g, span in zip(got, spans(width, dispatch_shares)):
        grad_lora += dot(g, down_out[:, span], 1, 1)
        grad_hidden += dot(g, down_w[:, span], 1, 1)
        down_grad.append((scale * dot(down_lora, g, 0, 0)).astype(bf))
    grad_lora = grad_lora.astype(bf)
    grad_hidden += scale * dot(grad_lora, down_in, 1, 0)
    grad_gate = (grad_hidden * up_v * sig * (1.0 + gate_v * (1.0 - sig))).astype(bf)
    grad_up = (grad_hidden * silu).astype(bf)
    gate_back = dot(grad_gate, gate_out, 1, 1).astype(bf)
    up_back = dot(grad_up, up_out, 1, 1).astype(bf)
    back = jnp.concatenate([gate_back, up_back], axis=1)
    left = jnp.concatenate([grad_gate, grad_up, back], axis=1)

    grad_in, before, lora, spread = [], None, None, None
    spare = jnp.zeros((slots, 128 - 2 * rank), bf)
    for at, span in enumerate(spans(width, return_shares)):
        right = joined[span]
        if at == 0:
            right = jnp.concatenate([right, choose], axis=0)
        rows_out = dot(left, right, 1, 1).astype(bf)
        if at == 2:
            rows_out = jnp.concatenate([rows_out, lora, spare], axis=1)
        if before is not None:
            rows_out, _ = lax.optimization_barrier((rows_out, before))
        before = exchange(rows_out.reshape(nc, rows, -1))
        wide = span.stop - span.start
        returned = before[:, :, :wide].reshape(slots, wide)
        partial = dot(pick.reshape(slots, ne * tok), returned, 0, 0).astype(bf)
        grad_in.append(lax.psum_scatter(partial, "ep", scatter_dimension=0, tiled=True))
        if at == 0:
            back_tok = before[:, :, wide : wide + 2 * rank]
            xs, _ = lax.optimization_barrier((xs, before))
            x_all = jnp.concatenate(xs, axis=0)
            block_of = (me + jnp.arange(ne, dtype=i32)) % ne
            lora_tok = dot(x_all, both_all, 1, 1).astype(bf).reshape(ne, tok, nc * 2 * rank)
            lora_tok = lora_tok[(jnp.arange(ne, dtype=i32) - me) % ne].reshape(ne * tok, nc, 2 * rank)
            lora = jnp.einsum("jrt,tji->jri", pick, lora_tok, preferred_element_type=f32)
            lora = lora.astype(bf).reshape(slots, 2 * rank)
            spread = jnp.einsum("jri,jrt->jit", back_tok, pick, preferred_element_type=f32).astype(bf)
            spread = spread.reshape(nc * 2 * rank, ne, tok)[:, block_of]
            share = scale * dot(spread.reshape(nc * 2 * rank, ne * tok), x_all, 1, 0)
            both_input_gradients = spread_sum(share.reshape(nc, 2 * rank, width), col)
        if at == 2:
            lora = before[:, :, wide : wide + 2 * rank].reshape(slots, 2 * rank)
            gate_output_gradient = (scale * dot(lora[:, :rank], grad_gate, 0, 0)).astype(bf)
            up_output_gradient = (scale * dot(lora[:, rank:], grad_up, 0, 0)).astype(bf)
    grad_in = jnp.concatenate(grad_in, axis=1)
    return (
        grad_in,
        both_input_gradients[None, :rank],
        gate_output_gradient[None],
        both_input_gradients[None, rank:],
        up_output_gradient[None],
        (scale * dot(grad_lora, hidden, 0, 0)).astype(bf)[None],
        jnp.concatenate(down_grad, axis=1)[None],
    )


def solution(mesh):
    flat, deep = P(("ctx", "ep"), None), P(("ctx", "ep"), None, None)
    return jax.shard_map(
        local,
        mesh=mesh,
        in_specs=(flat,) * 4 + (deep,) * 11,
        out_specs=(flat,) + (deep,) * 6,
        check_vma=False,
    )
```

```python
import jax
import jax.numpy as jnp
from jax import lax
from jax.sharding import PartitionSpec as P

scale = 2.0
dispatch_shares = (1, 1, 1, 1)
return_shares = (3, 5, 5, 3)
bf, f32, i32 = jnp.bfloat16, jnp.float32, jnp.int32


def dot(a, b, da, db):
    return lax.dot_general(
        a, b, (((da,), (db,)), ((), ())), preferred_element_type=jnp.float32
    )


def spread_sum(value, col):
    nc = value.shape[0]
    half = value.reshape(nc // 2, 2, *value.shape[1:])
    keep = lax.dynamic_index_in_dim(half, col % 2, 1, keepdims=False)
    give = lax.dynamic_index_in_dim(half, 1 - col % 2, 1, keepdims=False).astype(bf)
    keep = keep + lax.ppermute(give, "ctx", [(c, c ^ 1) for c in range(nc)]).astype(f32)
    total = lax.dynamic_index_in_dim(keep, col // 2, 0, keepdims=False)
    for j in range(1, nc // 2):
        out = lax.dynamic_index_in_dim(keep, col // 2 ^ j, 0, keepdims=False).astype(bf)
        total += lax.ppermute(out, "ctx", [(c, c ^ 2 * j) for c in range(nc)]).astype(f32)
    return total.astype(bf)


def spans(width, shares):
    unit, at = width // sum(shares), 0
    for share in shares:
        yield slice(at * unit, (at + share) * unit)
        at += share


def local(
    x,
    grad,
    ids,
    weights,
    gate_w,
    up_w,
    down_w,
    gate_in,
    gate_out,
    up_in,
    up_out,
    down_in,
    down_out,
    gate_pre,
    up_pre,
):
    gate_w, up_w, down_w = gate_w[0], up_w[0], down_w[0]
    gate_in, gate_out, up_in, up_out = gate_in[0], gate_out[0], up_in[0], up_out[0]
    down_in, down_out, gate_pre, up_pre = down_in[0], down_out[0], gate_pre[0], up_pre[0]
    tok, width = x.shape
    rank = gate_in.shape[0]
    nc, ne = lax.axis_size("ctx"), lax.axis_size("ep")
    slots = gate_pre.shape[0]
    rows = slots // nc
    cap = rows // ne
    top = ids.shape[1]
    col, me = lax.axis_index("ctx"), lax.axis_index("ep")

    def hop(value, step):
        return lax.ppermute(value, "ep", [((e + step) % ne, e) for e in range(ne)])

    def exchange(value):
        return lax.all_to_all(value, "ctx", split_axis=0, concat_axis=0, tiled=True)

    both_in = jnp.concatenate([gate_in, up_in], axis=0)
    both_all = exchange(jnp.broadcast_to(both_in, (nc,) + both_in.shape))
    both_all = both_all.reshape(nc * 2 * rank, width)
    packed = jnp.concatenate([ids.astype(f32), weights], axis=1)
    metas = lax.all_gather(packed, "ep")
    mine = jnp.arange(nc, dtype=i32) * ne + me
    chosen = metas[:, :, :top].astype(i32)
    hit = chosen[:, :, None, :] == mine[None, None, :, None]
    sel = jnp.any(hit, axis=3)
    wt = jnp.sum(jnp.where(hit, metas[:, :, None, top:], 0.0), axis=3)
    iota = jnp.arange(tok, dtype=i32)
    lower = (iota[:, None] > iota[None, :]).astype(bf)
    place = jnp.einsum("ts,esc->cet", lower, sel.astype(bf), preferred_element_type=f32)
    key = place.astype(i32) + (jnp.arange(ne, dtype=i32) * cap)[None, :, None]
    key = jnp.where(jnp.transpose(sel, (2, 0, 1)), key, -1).reshape(nc, 1, ne * tok)
    wt = jnp.transpose(wt, (2, 0, 1)).reshape(nc, 1, ne * tok)
    match = key == jnp.arange(rows, dtype=i32)[None, :, None]
    pick = match.astype(bf)
    slot_w = jnp.sum(jnp.where(match, wt, 0.0), axis=2, keepdims=True)

    got, blocks = [], []
    for span in spans(width, dispatch_shares):
        own = grad[:, span]
        if len(blocks) > 1:
            own, blocks[-2] = lax.optimization_barrier((own, blocks[-2]))
        blocks.append(lax.all_gather(own, "ep", tiled=True))
    for block in blocks:
        sent = (dot(pick, block, 2, 0) * slot_w).astype(bf)
        if got:
            sent, got[-1] = lax.optimization_barrier((sent, got[-1]))
        else:
            sent, both_all = lax.optimization_barrier((sent, both_all))
            first = sent
        got.append(exchange(sent))
    got = [g.reshape(slots, -1) for g in got]

    late_in, gate_pre, up_pre, gate_w, up_w, gate_out, up_out, _ = lax.optimization_barrier(
        (both_in, gate_pre, up_pre, gate_w, up_w, gate_out, up_out, first)
    )
    inner = gate_w.shape[1]
    gap = jnp.zeros_like(gate_out)
    both_out = jnp.concatenate(
        [jnp.concatenate([gate_out, gap], axis=1), jnp.concatenate([gap, up_out], axis=1)], axis=0
    )
    ride = jnp.arange(128, dtype=i32)[None, :] == jnp.arange(2 * rank, dtype=i32)[:, None]
    ride = ride.astype(bf)
    scaled_in = (late_in.astype(f32) * scale).astype(bf)
    mains, adds = [], []
    for at, span in enumerate(spans(width, return_shares)):
        main = jnp.concatenate([gate_w[span], up_w[span]], axis=1)
        add = scaled_in[:, span]
        wide = add.shape[1]
        if at in (0, 2):
            main = jnp.pad(main, ((0, 128), (0, 0)))
        if at == 0:
            add = jnp.concatenate([add, ride], axis=1)
        if at == 2:
            add = jnp.pad(add, ((0, 0), (0, 128)))
            lora_ride = jnp.pad(ride, ((0, 0), (wide, 0)))
        mains.append(main)
        adds.append(add)
    late_x, _ = lax.optimization_barrier((x, tuple(blocks)))
    xs = [x] + [hop(late_x, k) for k in range(1, ne)]

    gate_v, up_v = gate_pre.astype(f32), up_pre.astype(f32)
    sig = jax.nn.sigmoid(gate_v)
    silu = gate_v * sig
    hidden = (silu * up_v).astype(bf)
    factor = jnp.concatenate([up_v * sig * (1.0 + gate_v * (1.0 - sig)), silu], axis=1)
    factor, got[-1] = lax.optimization_barrier((factor, got[-1]))
    down_lora = dot(hidden, down_in, 1, 1).astype(bf)
    grad_lora, grad_hidden, down_grad = 0.0, 0.0, []
    for g, span in zip(got, spans(width, dispatch_shares)):
        grad_lora += dot(g, down_out[:, span], 1, 1)
        grad_hidden += dot(g, down_w[:, span], 1, 1)
        down_grad.append((scale * dot(down_lora, g, 0, 0)).astype(bf))
    grad_lora = grad_lora.astype(bf)
    grad_hidden += scale * dot(grad_lora, down_in, 1, 0)
    pair = (jnp.concatenate([grad_hidden, grad_hidden], axis=1) * factor).astype(bf)
    back = dot(pair, both_out, 1, 1).astype(bf)

    grad_in, before, lora, spread = [], None, None, None
    for at, span in enumerate(spans(width, return_shares)):
        rows_out = dot(pair, mains[at], 1, 1) + dot(back, adds[at], 1, 0)
        if at == 2:
            rows_out += dot(lora, lora_ride, 1, 0)
        rows_out = rows_out.astype(bf)
        if before is not None:
            rows_out, _ = lax.optimization_barrier((rows_out, before))
        before = exchange(rows_out.reshape(nc, rows, -1))
        wide = span.stop - span.start
        returned = before[:, :, :wide].reshape(slots, wide)
        partial = dot(pick.reshape(slots, ne * tok), returned, 0, 0).astype(bf)
        grad_in.append(lax.psum_scatter(partial, "ep", scatter_dimension=0, tiled=True))
        if at == 0:
            back_tok = before[:, :, wide : wide + 2 * rank]
            xs, _ = lax.optimization_barrier((xs, before))
            x_all = jnp.concatenate(xs, axis=0)
            block_of = (me + jnp.arange(ne, dtype=i32)) % ne
            lora_tok = dot(x_all, both_all, 1, 1).astype(bf).reshape(ne, tok, nc * 2 * rank)
            lora_tok = lora_tok[(jnp.arange(ne, dtype=i32) - me) % ne].reshape(ne * tok, nc, 2 * rank)
            lora = jnp.einsum("jrt,tji->jri", pick, lora_tok, preferred_element_type=f32)
            lora = lora.astype(bf).reshape(slots, 2 * rank)
            spread = jnp.einsum("jri,jrt->jit", back_tok, pick, preferred_element_type=f32).astype(bf)
            spread = spread.reshape(nc * 2 * rank, ne, tok)[:, block_of]
            share = scale * dot(spread.reshape(nc * 2 * rank, ne * tok), x_all, 1, 0)
            both_input_gradients = spread_sum(share.reshape(nc, 2 * rank, width), col)
        if at == 2:
            lora = before[:, :, wide : wide + 2 * rank].reshape(slots, 2 * rank)
            gate_output_gradient = (scale * dot(lora[:, :rank], pair[:, :inner], 0, 0)).astype(bf)
            up_output_gradient = (scale * dot(lora[:, rank:], pair[:, inner:], 0, 0)).astype(bf)
    grad_in = jnp.concatenate(grad_in, axis=1)
    return (
        grad_in,
        both_input_gradients[None, :rank],
        gate_output_gradient[None],
        both_input_gradients[None, rank:],
        up_output_gradient[None],
        (scale * dot(grad_lora, hidden, 0, 0)).astype(bf)[None],
        jnp.concatenate(down_grad, axis=1)[None],
    )


def solution(mesh):
    flat, deep = P(("ctx", "ep"), None), P(("ctx", "ep"), None, None)
    return jax.shard_map(
        local,
        mesh=mesh,
        in_specs=(flat,) * 4 + (deep,) * 11,
        out_specs=(flat,) + (deep,) * 6,
        check_vma=False,
    )
```

```python
import jax
import jax.numpy as jnp
from jax import lax
from jax.sharding import PartitionSpec as P

scale = 2.0
dispatch_shares = (4, 5, 7)
return_shares = (6, 6, 4)
bf, f32, i32 = jnp.bfloat16, jnp.float32, jnp.int32


def dot(a, b, da, db):
    return lax.dot_general(
        a, b, (((da,), (db,)), ((), ())), preferred_element_type=jnp.float32
    )


def spread_sum(value, col):
    nc = value.shape[0]
    half = value.reshape(nc // 2, 2, *value.shape[1:])
    keep = lax.dynamic_index_in_dim(half, col % 2, 1, keepdims=False)
    give = lax.dynamic_index_in_dim(half, 1 - col % 2, 1, keepdims=False).astype(bf)
    keep = keep + lax.ppermute(give, "ctx", [(c, c ^ 1) for c in range(nc)]).astype(f32)
    total = lax.dynamic_index_in_dim(keep, col // 2, 0, keepdims=False)
    for j in range(1, nc // 2):
        out = lax.dynamic_index_in_dim(keep, col // 2 ^ j, 0, keepdims=False).astype(bf)
        total += lax.ppermute(out, "ctx", [(c, c ^ 2 * j) for c in range(nc)]).astype(f32)
    return total.astype(bf)


def spans(width, shares):
    unit, at = width // sum(shares), 0
    for share in shares:
        yield slice(at * unit, (at + share) * unit)
        at += share


def local(
    x,
    grad,
    ids,
    weights,
    gate_w,
    up_w,
    down_w,
    gate_in,
    gate_out,
    up_in,
    up_out,
    down_in,
    down_out,
    gate_pre,
    up_pre,
):
    gate_w, up_w, down_w = gate_w[0], up_w[0], down_w[0]
    gate_in, gate_out, up_in, up_out = gate_in[0], gate_out[0], up_in[0], up_out[0]
    down_in, down_out, gate_pre, up_pre = down_in[0], down_out[0], gate_pre[0], up_pre[0]
    tok, width = x.shape
    rank = gate_in.shape[0]
    nc, ne = lax.axis_size("ctx"), lax.axis_size("ep")
    slots = gate_pre.shape[0]
    rows = slots // nc
    cap = rows // ne
    top = ids.shape[1]
    col, me = lax.axis_index("ctx"), lax.axis_index("ep")

    def hop(value, step):
        return lax.ppermute(value, "ep", [((e + step) % ne, e) for e in range(ne)])

    def exchange(value):
        return lax.all_to_all(value, "ctx", split_axis=0, concat_axis=0, tiled=True)

    packed = jnp.concatenate([ids.astype(f32), weights], axis=1)
    metas = lax.all_gather(packed, "ep")
    mine = jnp.arange(nc, dtype=i32) * ne + me
    chosen = metas[:, :, :top].astype(i32)
    hit = chosen[:, :, None, :] == mine[None, None, :, None]
    sel = jnp.any(hit, axis=3)
    wt = jnp.sum(jnp.where(hit, metas[:, :, None, top:], 0.0), axis=3)
    iota = jnp.arange(tok, dtype=i32)
    lower = (iota[:, None] > iota[None, :]).astype(bf)
    place = jnp.einsum("ts,esc->cet", lower, sel.astype(bf), preferred_element_type=f32)
    key = place.astype(i32) + (jnp.arange(ne, dtype=i32) * cap)[None, :, None]
    key = jnp.where(jnp.transpose(sel, (2, 0, 1)), key, -1).reshape(nc, 1, ne * tok)
    wt = jnp.transpose(wt, (2, 0, 1)).reshape(nc, 1, ne * tok)
    match = key == jnp.arange(rows, dtype=i32)[None, :, None]
    pick = match.astype(bf)
    slot_w = jnp.sum(jnp.where(match, wt, 0.0), axis=2, keepdims=True)

    got, blocks = [], []
    for span in spans(width, dispatch_shares):
        own = grad[:, span]
        if len(blocks) > 1:
            own, blocks[-2] = lax.optimization_barrier((own, blocks[-2]))
        blocks.append(lax.all_gather(own, "ep", tiled=True))
    for block in blocks:
        sent = (dot(pick, block, 2, 0) * slot_w).astype(bf)
        if got:
            sent, got[-1] = lax.optimization_barrier((sent, got[-1]))
        else:
            first = sent
        got.append(exchange(sent))
    got = [g.reshape(slots, -1) for g in got]

    both_in, gate_pre, up_pre, late_gate, late_up, _ = lax.optimization_barrier(
        (jnp.concatenate([gate_in, up_in], axis=0), gate_pre, up_pre, gate_w, up_w, first)
    )
    scaled_in = (both_in.astype(f32) * scale).astype(bf)
    joined = jnp.concatenate([late_gate, late_up, scaled_in.T], axis=1)
    inner = 2 * gate_w.shape[1]
    choose = (
        jnp.arange(128, dtype=i32)[:, None] + inner == jnp.arange(inner + 2 * rank, dtype=i32)[None, :]
    ).astype(bf)
    late_x, late_in, _ = lax.optimization_barrier((x, both_in, tuple(blocks)))
    xs = [x] + [hop(late_x, k) for k in range(1, ne)]
    both_all = lax.all_gather(late_in, "ctx", tiled=True)

    gate_v, up_v = gate_pre.astype(f32), up_pre.astype(f32)
    sig = jax.nn.sigmoid(gate_v)
    silu = gate_v * sig
    hidden = (silu * up_v).astype(bf)
    down_lora = dot(hidden, down_in, 1, 1).astype(bf)
    grad_lora, grad_hidden, down_grad = 0.0, 0.0, []
    for g, span in zip(got, spans(width, dispatch_shares)):
        grad_lora += dot(g, down_out[:, span], 1, 1)
        grad_hidden += dot(g, down_w[:, span], 1, 1)
        down_grad.append((scale * dot(down_lora, g, 0, 0)).astype(bf))
    grad_lora = grad_lora.astype(bf)
    grad_hidden += scale * dot(grad_lora, down_in, 1, 0)
    grad_gate = (grad_hidden * up_v * sig * (1.0 + gate_v * (1.0 - sig))).astype(bf)
    grad_up = (grad_hidden * silu).astype(bf)
    gate_back = dot(grad_gate, gate_out, 1, 1).astype(bf)
    up_back = dot(grad_up, up_out, 1, 1).astype(bf)
    back = jnp.concatenate([gate_back, up_back], axis=1)
    left = jnp.concatenate([grad_gate, grad_up, back], axis=1)

    grad_in, before, lora, spread = [], None, None, None
    ride = jnp.arange(128, dtype=i32)[None, :] == jnp.arange(2 * rank, dtype=i32)[:, None]
    for at, span in enumerate(spans(width, return_shares)):
        right = joined[span]
        if at == 0:
            right = jnp.concatenate([right, choose], axis=0)
        if at == 1:
            right = jnp.pad(right, ((0, 128), (0, 0)))
        rows_out = dot(left, right, 1, 1)
        if at == 1:
            rider = jnp.pad(ride.astype(bf), ((0, 0), (span.stop - span.start, 0)))
            rows_out += dot(lora, rider, 1, 0)
        rows_out = rows_out.astype(bf)
        if before is not None:
            rows_out, _ = lax.optimization_barrier((rows_out, before))
        before = exchange(rows_out.reshape(nc, rows, -1))
        wide = span.stop - span.start
        returned = before[:, :, :wide].reshape(slots, wide)
        partial = dot(pick.reshape(slots, ne * tok), returned, 0, 0).astype(bf)
        grad_in.append(lax.psum_scatter(partial, "ep", scatter_dimension=0, tiled=True))
        if at == 0:
            back_tok = before[:, :, wide : wide + 2 * rank]
            xs, _ = lax.optimization_barrier((xs, before))
            x_all = jnp.concatenate(xs, axis=0)
            block_of = (me + jnp.arange(ne, dtype=i32)) % ne
            lora_tok = dot(x_all, both_all, 1, 1).astype(bf).reshape(ne, tok, nc * 2 * rank)
            lora_tok = lora_tok[(jnp.arange(ne, dtype=i32) - me) % ne].reshape(ne * tok, nc, 2 * rank)
            lora = jnp.einsum("jrt,tji->jri", pick, lora_tok, preferred_element_type=f32)
            lora = lora.astype(bf).reshape(slots, 2 * rank)
            spread = jnp.einsum("jri,jrt->jit", back_tok, pick, preferred_element_type=f32).astype(bf)
            spread = spread.reshape(nc * 2 * rank, ne, tok)[:, block_of]
            share = scale * dot(spread.reshape(nc * 2 * rank, ne * tok), x_all, 1, 0)
            both_input_gradients = spread_sum(share.reshape(nc, 2 * rank, width), col)
        if at == 1:
            lora = before[:, :, wide : wide + 2 * rank].reshape(slots, 2 * rank)
            gate_output_gradient = (scale * dot(lora[:, :rank], grad_gate, 0, 0)).astype(bf)
            up_output_gradient = (scale * dot(lora[:, rank:], grad_up, 0, 0)).astype(bf)
    grad_in = jnp.concatenate(grad_in, axis=1)
    return (
        grad_in,
        both_input_gradients[None, :rank],
        gate_output_gradient[None],
        both_input_gradients[None, rank:],
        up_output_gradient[None],
        (scale * dot(grad_lora, hidden, 0, 0)).astype(bf)[None],
        jnp.concatenate(down_grad, axis=1)[None],
    )


def solution(mesh):
    flat, deep = P(("ctx", "ep"), None), P(("ctx", "ep"), None, None)
    return jax.shard_map(
        local,
        mesh=mesh,
        in_specs=(flat,) * 4 + (deep,) * 11,
        out_specs=(flat,) + (deep,) * 6,
        check_vma=False,
    )
```

```python
import jax
import jax.numpy as jnp
from jax import lax
from jax.sharding import PartitionSpec as P

scale = 2.0
dispatch_shares = (4, 5, 7)
return_shares = (4, 7, 5)
bf, f32, i32 = jnp.bfloat16, jnp.float32, jnp.int32


def dot(a, b, da, db):
    return lax.dot_general(
        a, b, (((da,), (db,)), ((), ())), preferred_element_type=jnp.float32
    )


def spread_sum(value, col):
    nc = value.shape[0]
    half = value.reshape(nc // 2, 2, *value.shape[1:])
    keep = lax.dynamic_index_in_dim(half, col % 2, 1, keepdims=False)
    give = lax.dynamic_index_in_dim(half, 1 - col % 2, 1, keepdims=False).astype(bf)
    keep = keep + lax.ppermute(give, "ctx", [(c, c ^ 1) for c in range(nc)]).astype(f32)
    total = lax.dynamic_index_in_dim(keep, col // 2, 0, keepdims=False)
    for j in range(1, nc // 2):
        out = lax.dynamic_index_in_dim(keep, col // 2 ^ j, 0, keepdims=False).astype(bf)
        total += lax.ppermute(out, "ctx", [(c, c ^ 2 * j) for c in range(nc)]).astype(f32)
    return total.astype(bf)


def spans(width, shares):
    unit, at = width // sum(shares), 0
    for share in shares:
        yield slice(at * unit, (at + share) * unit)
        at += share


def local(
    x,
    grad,
    ids,
    weights,
    gate_w,
    up_w,
    down_w,
    gate_in,
    gate_out,
    up_in,
    up_out,
    down_in,
    down_out,
    gate_pre,
    up_pre,
):
    gate_w, up_w, down_w = gate_w[0], up_w[0], down_w[0]
    gate_in, gate_out, up_in, up_out = gate_in[0], gate_out[0], up_in[0], up_out[0]
    down_in, down_out, gate_pre, up_pre = down_in[0], down_out[0], gate_pre[0], up_pre[0]
    tok, width = x.shape
    rank = gate_in.shape[0]
    nc, ne = lax.axis_size("ctx"), lax.axis_size("ep")
    slots = gate_pre.shape[0]
    rows = slots // nc
    cap = rows // ne
    top = ids.shape[1]
    col, me = lax.axis_index("ctx"), lax.axis_index("ep")

    def hop(value, step):
        return lax.ppermute(value, "ep", [((e + step) % ne, e) for e in range(ne)])

    def exchange(value):
        return lax.all_to_all(value, "ctx", split_axis=0, concat_axis=0, tiled=True)

    packed = jnp.concatenate([ids.astype(f32), weights], axis=1)
    metas = lax.all_gather(packed, "ep")
    mine = jnp.arange(nc, dtype=i32) * ne + me
    chosen = metas[:, :, :top].astype(i32)
    hit = chosen[:, :, None, :] == mine[None, None, :, None]
    sel = jnp.any(hit, axis=3)
    wt = jnp.sum(jnp.where(hit, metas[:, :, None, top:], 0.0), axis=3)
    iota = jnp.arange(tok, dtype=i32)
    lower = (iota[:, None] > iota[None, :]).astype(bf)
    place = jnp.einsum("ts,esc->cet", lower, sel.astype(bf), preferred_element_type=f32)
    key = place.astype(i32) + (jnp.arange(ne, dtype=i32) * cap)[None, :, None]
    key = jnp.where(jnp.transpose(sel, (2, 0, 1)), key, -1).reshape(nc, 1, ne * tok)
    wt = jnp.transpose(wt, (2, 0, 1)).reshape(nc, 1, ne * tok)
    match = key == jnp.arange(rows, dtype=i32)[None, :, None]
    pick = match.astype(bf)
    slot_w = jnp.sum(jnp.where(match, wt, 0.0), axis=2, keepdims=True)

    got, blocks = [], []
    for span in spans(width, dispatch_shares):
        own = grad[:, span]
        if len(blocks) > 1:
            own, blocks[-2] = lax.optimization_barrier((own, blocks[-2]))
        blocks.append(lax.all_gather(own, "ep", tiled=True))
    for block in blocks:
        sent = (dot(pick, block, 2, 0) * slot_w).astype(bf)
        if got:
            sent, got[-1] = lax.optimization_barrier((sent, got[-1]))
        else:
            first = sent
        got.append(exchange(sent))
    got = [g.reshape(slots, -1) for g in got]

    both_in, gate_pre, up_pre, late_gate, late_up, _ = lax.optimization_barrier(
        (jnp.concatenate([gate_in, up_in], axis=0), gate_pre, up_pre, gate_w, up_w, first)
    )
    scaled_in = (both_in.astype(f32) * scale).astype(bf)
    joined = jnp.concatenate([late_gate, late_up, scaled_in.T], axis=1)
    inner = 2 * gate_w.shape[1]
    choose = (
        jnp.arange(128, dtype=i32)[:, None] + inner == jnp.arange(inner + 2 * rank, dtype=i32)[None, :]
    ).astype(bf)
    late_x, late_in, _ = lax.optimization_barrier((x, both_in, tuple(blocks)))
    xs = [x] + [hop(late_x, k) for k in range(1, ne)]
    both_all = lax.all_gather(late_in, "ctx", tiled=True)

    gate_v, up_v = gate_pre.astype(f32), up_pre.astype(f32)
    sig = jax.nn.sigmoid(gate_v)
    silu = gate_v * sig
    hidden = (silu * up_v).astype(bf)
    down_lora = dot(hidden, down_in, 1, 1).astype(bf)
    grad_lora, grad_hidden, down_grad = 0.0, 0.0, []
    for g, span in zip(got, spans(width, dispatch_shares)):
        grad_lora += dot(g, down_out[:, span], 1, 1)
        grad_hidden += dot(g, down_w[:, span], 1, 1)
        down_grad.append((scale * dot(down_lora, g, 0, 0)).astype(bf))
    grad_lora = grad_lora.astype(bf)
    grad_hidden += scale * dot(grad_lora, down_in, 1, 0)
    grad_gate = (grad_hidden * up_v * sig * (1.0 + gate_v * (1.0 - sig))).astype(bf)
    grad_up = (grad_hidden * silu).astype(bf)
    gate_back = dot(grad_gate, gate_out, 1, 1).astype(bf)
    up_back = dot(grad_up, up_out, 1, 1).astype(bf)
    back = jnp.concatenate([gate_back, up_back], axis=1)
    left = jnp.concatenate([grad_gate, grad_up, back], axis=1)

    grad_in, before, lora, spread = [], None, None, None
    ride = jnp.arange(128, dtype=i32)[None, :] == jnp.arange(2 * rank, dtype=i32)[:, None]
    for at, span in enumerate(spans(width, return_shares)):
        right = joined[span]
        if at == 0:
            right = jnp.concatenate([right, choose], axis=0)
        if at == 2:
            right = jnp.pad(right, ((0, 128), (0, 0)))
        rows_out = dot(left, right, 1, 1)
        if at == 2:
            rider = jnp.pad(ride.astype(bf), ((0, 0), (span.stop - span.start, 0)))
            rows_out += dot(lora, rider, 1, 0)
        rows_out = rows_out.astype(bf)
        if before is not None:
            rows_out, _ = lax.optimization_barrier((rows_out, before))
        before = exchange(rows_out.reshape(nc, rows, -1))
        wide = span.stop - span.start
        returned = before[:, :, :wide].reshape(slots, wide)
        partial = dot(pick.reshape(slots, ne * tok), returned, 0, 0).astype(bf)
        grad_in.append(lax.psum_scatter(partial, "ep", scatter_dimension=0, tiled=True))
        if at == 0:
            back_tok = before[:, :, wide : wide + 2 * rank]
            xs, _ = lax.optimization_barrier((xs, before))
            x_all = jnp.concatenate(xs, axis=0)
            block_of = (me + jnp.arange(ne, dtype=i32)) % ne
            lora_tok = dot(x_all, both_all, 1, 1).astype(bf).reshape(ne, tok, nc * 2 * rank)
            lora_tok = lora_tok[(jnp.arange(ne, dtype=i32) - me) % ne].reshape(ne * tok, nc, 2 * rank)
            lora = jnp.einsum("jrt,tji->jri", pick, lora_tok, preferred_element_type=f32)
            lora = lora.astype(bf).reshape(slots, 2 * rank)
            spread = jnp.einsum("jri,jrt->jit", back_tok, pick, preferred_element_type=f32).astype(bf)
            spread = spread.reshape(nc * 2 * rank, ne, tok)[:, block_of]
            share = scale * dot(spread.reshape(nc * 2 * rank, ne * tok), x_all, 1, 0)
            both_input_gradients = spread_sum(share.reshape(nc, 2 * rank, width), col)
        if at == 2:
            lora = before[:, :, wide : wide + 2 * rank].reshape(slots, 2 * rank)
            gate_output_gradient = (scale * dot(lora[:, :rank], grad_gate, 0, 0)).astype(bf)
            up_output_gradient = (scale * dot(lora[:, rank:], grad_up, 0, 0)).astype(bf)
    grad_in = jnp.concatenate(grad_in, axis=1)
    return (
        grad_in,
        both_input_gradients[None, :rank],
        gate_output_gradient[None],
        both_input_gradients[None, rank:],
        up_output_gradient[None],
        (scale * dot(grad_lora, hidden, 0, 0)).astype(bf)[None],
        jnp.concatenate(down_grad, axis=1)[None],
    )


def solution(mesh):
    flat, deep = P(("ctx", "ep"), None), P(("ctx", "ep"), None, None)
    return jax.shard_map(
        local,
        mesh=mesh,
        in_specs=(flat,) * 4 + (deep,) * 11,
        out_specs=(flat,) + (deep,) * 6,
        check_vma=False,
    )
```

```python
import jax
import jax.numpy as jnp
from jax import lax
from jax.sharding import PartitionSpec as P

scale = 2.0
dispatch_shares = (4, 5, 7)
return_shares = (4, 7, 5)
bf, f32, i32 = jnp.bfloat16, jnp.float32, jnp.int32


def dot(a, b, da, db):
    return lax.dot_general(
        a, b, (((da,), (db,)), ((), ())), preferred_element_type=jnp.float32
    )


def spread_sum(value, col):
    nc = value.shape[0]
    half = value.reshape(nc // 2, 2, *value.shape[1:])
    keep = lax.dynamic_index_in_dim(half, col % 2, 1, keepdims=False)
    give = lax.dynamic_index_in_dim(half, 1 - col % 2, 1, keepdims=False).astype(bf)
    keep = keep + lax.ppermute(give, "ctx", [(c, c ^ 1) for c in range(nc)]).astype(f32)
    total = lax.dynamic_index_in_dim(keep, col // 2, 0, keepdims=False)
    for j in range(1, nc // 2):
        out = lax.dynamic_index_in_dim(keep, col // 2 ^ j, 0, keepdims=False).astype(bf)
        total += lax.ppermute(out, "ctx", [(c, c ^ 2 * j) for c in range(nc)]).astype(f32)
    return total.astype(bf)


def spans(width, shares):
    unit, at = width // sum(shares), 0
    for share in shares:
        yield slice(at * unit, (at + share) * unit)
        at += share


def local(
    x,
    grad,
    ids,
    weights,
    gate_w,
    up_w,
    down_w,
    gate_in,
    gate_out,
    up_in,
    up_out,
    down_in,
    down_out,
    gate_pre,
    up_pre,
):
    gate_w, up_w, down_w = gate_w[0], up_w[0], down_w[0]
    gate_in, gate_out, up_in, up_out = gate_in[0], gate_out[0], up_in[0], up_out[0]
    down_in, down_out, gate_pre, up_pre = down_in[0], down_out[0], gate_pre[0], up_pre[0]
    tok, width = x.shape
    rank = gate_in.shape[0]
    nc, ne = lax.axis_size("ctx"), lax.axis_size("ep")
    slots = gate_pre.shape[0]
    rows = slots // nc
    cap = rows // ne
    top = ids.shape[1]
    col, me = lax.axis_index("ctx"), lax.axis_index("ep")

    def hop(value, step):
        return lax.ppermute(value, "ep", [((e + step) % ne, e) for e in range(ne)])

    def exchange(value):
        return lax.all_to_all(value, "ctx", split_axis=0, concat_axis=0, tiled=True)

    packed = jnp.concatenate([ids.astype(f32), weights], axis=1)
    metas = lax.all_gather(packed, "ep")
    mine = jnp.arange(nc, dtype=i32) * ne + me
    chosen = metas[:, :, :top].astype(i32)
    hit = chosen[:, :, None, :] == mine[None, None, :, None]
    sel = jnp.any(hit, axis=3)
    wt = jnp.sum(jnp.where(hit, metas[:, :, None, top:], 0.0), axis=3)
    iota = jnp.arange(tok, dtype=i32)
    lower = (iota[:, None] > iota[None, :]).astype(bf)
    place = jnp.einsum("ts,esc->cet", lower, sel.astype(bf), preferred_element_type=f32)
    key = place.astype(i32) + (jnp.arange(ne, dtype=i32) * cap)[None, :, None]
    key = jnp.where(jnp.transpose(sel, (2, 0, 1)), key, -1).reshape(nc, 1, ne * tok)
    wt = jnp.transpose(wt, (2, 0, 1)).reshape(nc, 1, ne * tok)
    match = key == jnp.arange(rows, dtype=i32)[None, :, None]
    pick = match.astype(bf)
    slot_w = jnp.sum(jnp.where(match, wt, 0.0), axis=2, keepdims=True)

    got, blocks = [], []
    for span in spans(width, dispatch_shares):
        own = grad[:, span]
        if len(blocks) > 1:
            own, blocks[-2] = lax.optimization_barrier((own, blocks[-2]))
        blocks.append(lax.all_gather(own, "ep", tiled=True))
    for block in blocks:
        sent = (dot(pick, block, 2, 0) * slot_w).astype(bf)
        if got:
            sent, got[-1] = lax.optimization_barrier((sent, got[-1]))
        else:
            first = sent
        got.append(exchange(sent))
    got = [g.reshape(slots, -1) for g in got]

    both_in, gate_pre, up_pre, late_gate, late_up, _ = lax.optimization_barrier(
        (jnp.concatenate([gate_in, up_in], axis=0), gate_pre, up_pre, gate_w, up_w, first)
    )
    scaled_in = (both_in.astype(f32) * scale).astype(bf)
    joined = jnp.concatenate([late_gate, late_up, scaled_in.T], axis=1)
    inner = 2 * gate_w.shape[1]
    choose = (
        jnp.arange(128, dtype=i32)[:, None] + inner == jnp.arange(inner + 2 * rank, dtype=i32)[None, :]
    ).astype(bf)
    late_x, late_in, _ = lax.optimization_barrier((x, both_in, tuple(blocks)))
    xs = [x] + [hop(late_x, k) for k in range(1, ne)]
    both_all = lax.all_gather(late_in, "ctx", tiled=True)

    gate_v, up_v = gate_pre.astype(f32), up_pre.astype(f32)
    sig = jax.nn.sigmoid(gate_v)
    silu = gate_v * sig
    hidden = (silu * up_v).astype(bf)
    down_lora = dot(hidden, down_in, 1, 1).astype(bf)
    grad_lora, grad_hidden, down_grad = 0.0, 0.0, []
    for g, span in zip(got, spans(width, dispatch_shares)):
        grad_lora += dot(g, down_out[:, span], 1, 1)
        grad_hidden += dot(g, down_w[:, span], 1, 1)
        down_grad.append((scale * dot(down_lora, g, 0, 0)).astype(bf))
    grad_lora = grad_lora.astype(bf)
    grad_hidden += scale * dot(grad_lora, down_in, 1, 0)
    grad_gate = (grad_hidden * up_v * sig * (1.0 + gate_v * (1.0 - sig))).astype(bf)
    grad_up = (grad_hidden * silu).astype(bf)
    gate_back = dot(grad_gate, gate_out, 1, 1).astype(bf)
    up_back = dot(grad_up, up_out, 1, 1).astype(bf)
    back = jnp.concatenate([gate_back, up_back], axis=1)
    left = jnp.concatenate([grad_gate, grad_up, back], axis=1)

    grad_in, before, lora, spread = [], None, None, None
    ride = jnp.arange(128, dtype=i32)[None, :] == jnp.arange(2 * rank, dtype=i32)[:, None]
    for at, span in enumerate(spans(width, return_shares)):
        right = joined[span]
        if at == 1:
            right = jnp.concatenate([right, choose], axis=0)
        if at == 2:
            right = jnp.pad(right, ((0, 128), (0, 0)))
        rows_out = dot(left, right, 1, 1)
        if at == 2:
            rider = jnp.pad(ride.astype(bf), ((0, 0), (span.stop - span.start, 0)))
            rows_out += dot(lora, rider, 1, 0)
        rows_out = rows_out.astype(bf)
        if before is not None:
            rows_out, _ = lax.optimization_barrier((rows_out, before))
        before = exchange(rows_out.reshape(nc, rows, -1))
        wide = span.stop - span.start
        returned = before[:, :, :wide].reshape(slots, wide)
        partial = dot(pick.reshape(slots, ne * tok), returned, 0, 0).astype(bf)
        grad_in.append(lax.psum_scatter(partial, "ep", scatter_dimension=0, tiled=True))
        if at == 0:
            xs, _ = lax.optimization_barrier((xs, before))
            x_all = jnp.concatenate(xs, axis=0)
            block_of = (me + jnp.arange(ne, dtype=i32)) % ne
            lora_tok = dot(x_all, both_all, 1, 1).astype(bf).reshape(ne, tok, nc * 2 * rank)
            lora_tok = lora_tok[(jnp.arange(ne, dtype=i32) - me) % ne].reshape(ne * tok, nc, 2 * rank)
            lora = jnp.einsum("jrt,tji->jri", pick, lora_tok, preferred_element_type=f32)
            lora = lora.astype(bf).reshape(slots, 2 * rank)
        if at == 1:
            back_tok = before[:, :, wide : wide + 2 * rank]
            spread = jnp.einsum("jri,jrt->jit", back_tok, pick, preferred_element_type=f32).astype(bf)
            spread = spread.reshape(nc * 2 * rank, ne, tok)[:, block_of]
            share = scale * dot(spread.reshape(nc * 2 * rank, ne * tok), x_all, 1, 0)
            both_input_gradients = spread_sum(share.reshape(nc, 2 * rank, width), col)
        if at == 2:
            lora = before[:, :, wide : wide + 2 * rank].reshape(slots, 2 * rank)
            gate_output_gradient = (scale * dot(lora[:, :rank], grad_gate, 0, 0)).astype(bf)
            up_output_gradient = (scale * dot(lora[:, rank:], grad_up, 0, 0)).astype(bf)
    grad_in = jnp.concatenate(grad_in, axis=1)
    return (
        grad_in,
        both_input_gradients[None, :rank],
        gate_output_gradient[None],
        both_input_gradients[None, rank:],
        up_output_gradient[None],
        (scale * dot(grad_lora, hidden, 0, 0)).astype(bf)[None],
        jnp.concatenate(down_grad, axis=1)[None],
    )


def solution(mesh):
    flat, deep = P(("ctx", "ep"), None), P(("ctx", "ep"), None, None)
    return jax.shard_map(
        local,
        mesh=mesh,
        in_specs=(flat,) * 4 + (deep,) * 11,
        out_specs=(flat,) + (deep,) * 6,
        check_vma=False,
    )
```

```python
import jax
import jax.numpy as jnp
from jax import lax
from jax.sharding import PartitionSpec as P

scale = 2.0
dispatch_shares = (4, 5, 7)
return_shares = (7, 14, 11)
bf, f32, i32 = jnp.bfloat16, jnp.float32, jnp.int32


def dot(a, b, da, db):
    return lax.dot_general(
        a, b, (((da,), (db,)), ((), ())), preferred_element_type=jnp.float32
    )


def spread_sum(value, col):
    nc = value.shape[0]
    half = value.reshape(nc // 2, 2, *value.shape[1:])
    keep = lax.dynamic_index_in_dim(half, col % 2, 1, keepdims=False)
    give = lax.dynamic_index_in_dim(half, 1 - col % 2, 1, keepdims=False).astype(bf)
    keep = keep + lax.ppermute(give, "ctx", [(c, c ^ 1) for c in range(nc)]).astype(f32)
    total = lax.dynamic_index_in_dim(keep, col // 2, 0, keepdims=False)
    for j in range(1, nc // 2):
        out = lax.dynamic_index_in_dim(keep, col // 2 ^ j, 0, keepdims=False).astype(bf)
        total += lax.ppermute(out, "ctx", [(c, c ^ 2 * j) for c in range(nc)]).astype(f32)
    return total.astype(bf)


def spans(width, shares):
    unit, at = width // sum(shares), 0
    for share in shares:
        yield slice(at * unit, (at + share) * unit)
        at += share


def local(
    x,
    grad,
    ids,
    weights,
    gate_w,
    up_w,
    down_w,
    gate_in,
    gate_out,
    up_in,
    up_out,
    down_in,
    down_out,
    gate_pre,
    up_pre,
):
    gate_w, up_w, down_w = gate_w[0], up_w[0], down_w[0]
    gate_in, gate_out, up_in, up_out = gate_in[0], gate_out[0], up_in[0], up_out[0]
    down_in, down_out, gate_pre, up_pre = down_in[0], down_out[0], gate_pre[0], up_pre[0]
    tok, width = x.shape
    rank = gate_in.shape[0]
    nc, ne = lax.axis_size("ctx"), lax.axis_size("ep")
    slots = gate_pre.shape[0]
    rows = slots // nc
    cap = rows // ne
    top = ids.shape[1]
    col, me = lax.axis_index("ctx"), lax.axis_index("ep")

    def hop(value, step):
        return lax.ppermute(value, "ep", [((e + step) % ne, e) for e in range(ne)])

    def exchange(value):
        return lax.all_to_all(value, "ctx", split_axis=0, concat_axis=0, tiled=True)

    packed = jnp.concatenate([ids.astype(f32), weights], axis=1)
    metas = lax.all_gather(packed, "ep")
    mine = jnp.arange(nc, dtype=i32) * ne + me
    chosen = metas[:, :, :top].astype(i32)
    hit = chosen[:, :, None, :] == mine[None, None, :, None]
    sel = jnp.any(hit, axis=3)
    wt = jnp.sum(jnp.where(hit, metas[:, :, None, top:], 0.0), axis=3)
    iota = jnp.arange(tok, dtype=i32)
    lower = (iota[:, None] > iota[None, :]).astype(bf)
    place = jnp.einsum("ts,esc->cet", lower, sel.astype(bf), preferred_element_type=f32)
    key = place.astype(i32) + (jnp.arange(ne, dtype=i32) * cap)[None, :, None]
    key = jnp.where(jnp.transpose(sel, (2, 0, 1)), key, -1).reshape(nc, 1, ne * tok)
    wt = jnp.transpose(wt, (2, 0, 1)).reshape(nc, 1, ne * tok)
    match = key == jnp.arange(rows, dtype=i32)[None, :, None]
    pick = match.astype(bf)
    slot_w = jnp.sum(jnp.where(match, wt, 0.0), axis=2, keepdims=True)

    got, blocks = [], []
    for span in spans(width, dispatch_shares):
        own = grad[:, span]
        if len(blocks) > 1:
            own, blocks[-2] = lax.optimization_barrier((own, blocks[-2]))
        blocks.append(lax.all_gather(own, "ep", tiled=True))
    for block in blocks:
        sent = (dot(pick, block, 2, 0) * slot_w).astype(bf)
        if got:
            sent, got[-1] = lax.optimization_barrier((sent, got[-1]))
        else:
            first = sent
        got.append(exchange(sent))
    got = [g.reshape(slots, -1) for g in got]

    both_in, gate_pre, up_pre, late_gate, late_up, _ = lax.optimization_barrier(
        (jnp.concatenate([gate_in, up_in], axis=0), gate_pre, up_pre, gate_w, up_w, first)
    )
    scaled_in = (both_in.astype(f32) * scale).astype(bf)
    joined = jnp.concatenate([late_gate, late_up, scaled_in.T], axis=1)
    inner = 2 * gate_w.shape[1]
    choose = (
        jnp.arange(128, dtype=i32)[:, None] + inner == jnp.arange(inner + 2 * rank, dtype=i32)[None, :]
    ).astype(bf)
    late_x, late_in, _ = lax.optimization_barrier((x, both_in, tuple(blocks)))
    xs = [x] + [hop(late_x, k) for k in range(1, ne)]
    both_all = lax.all_gather(late_in, "ctx", tiled=True)

    gate_v, up_v = gate_pre.astype(f32), up_pre.astype(f32)
    sig = jax.nn.sigmoid(gate_v)
    silu = gate_v * sig
    hidden = (silu * up_v).astype(bf)
    down_lora = dot(hidden, down_in, 1, 1).astype(bf)
    grad_lora, grad_hidden, down_grad = 0.0, 0.0, []
    for g, span in zip(got, spans(width, dispatch_shares)):
        grad_lora += dot(g, down_out[:, span], 1, 1)
        grad_hidden += dot(g, down_w[:, span], 1, 1)
        down_grad.append((scale * dot(down_lora, g, 0, 0)).astype(bf))
    grad_lora = grad_lora.astype(bf)
    grad_hidden += scale * dot(grad_lora, down_in, 1, 0)
    grad_gate = (grad_hidden * up_v * sig * (1.0 + gate_v * (1.0 - sig))).astype(bf)
    grad_up = (grad_hidden * silu).astype(bf)
    gate_back = dot(grad_gate, gate_out, 1, 1).astype(bf)
    up_back = dot(grad_up, up_out, 1, 1).astype(bf)
    back = jnp.concatenate([gate_back, up_back], axis=1)
    left = jnp.concatenate([grad_gate, grad_up, back], axis=1)

    grad_in, before, lora, spread = [], None, None, None
    ride = jnp.arange(128, dtype=i32)[None, :] == jnp.arange(2 * rank, dtype=i32)[:, None]
    for at, span in enumerate(spans(width, return_shares)):
        right = joined[span]
        if at == 0:
            right = jnp.concatenate([right, choose], axis=0)
        if at == 2:
            right = jnp.pad(right, ((0, 128), (0, 0)))
        rows_out = dot(left, right, 1, 1)
        if at == 2:
            rider = jnp.pad(ride.astype(bf), ((0, 0), (span.stop - span.start, 0)))
            rows_out += dot(lora, rider, 1, 0)
        rows_out = rows_out.astype(bf)
        if before is not None:
            rows_out, _ = lax.optimization_barrier((rows_out, before))
        before = exchange(rows_out.reshape(nc, rows, -1))
        wide = span.stop - span.start
        returned = before[:, :, :wide].reshape(slots, wide)
        partial = dot(pick.reshape(slots, ne * tok), returned, 0, 0).astype(bf)
        grad_in.append(lax.psum_scatter(partial, "ep", scatter_dimension=0, tiled=True))
        if at == 0:
            back_tok = before[:, :, wide : wide + 2 * rank]
            xs, _ = lax.optimization_barrier((xs, before))
            x_all = jnp.concatenate(xs, axis=0)
            block_of = (me + jnp.arange(ne, dtype=i32)) % ne
            lora_tok = dot(x_all, both_all, 1, 1).astype(bf).reshape(ne, tok, nc * 2 * rank)
            lora_tok = lora_tok[(jnp.arange(ne, dtype=i32) - me) % ne].reshape(ne * tok, nc, 2 * rank)
            lora = jnp.einsum("jrt,tji->jri", pick, lora_tok, preferred_element_type=f32)
            lora = lora.astype(bf).reshape(slots, 2 * rank)
            spread = jnp.einsum("jri,jrt->jit", back_tok, pick, preferred_element_type=f32).astype(bf)
            spread = spread.reshape(nc * 2 * rank, ne, tok)[:, block_of]
            share = scale * dot(spread.reshape(nc * 2 * rank, ne * tok), x_all, 1, 0)
            both_input_gradients = spread_sum(share.reshape(nc, 2 * rank, width), col)
        if at == 2:
            lora = before[:, :, wide : wide + 2 * rank].reshape(slots, 2 * rank)
            gate_output_gradient = (scale * dot(lora[:, :rank], grad_gate, 0, 0)).astype(bf)
            up_output_gradient = (scale * dot(lora[:, rank:], grad_up, 0, 0)).astype(bf)
    grad_in = jnp.concatenate(grad_in, axis=1)
    return (
        grad_in,
        both_input_gradients[None, :rank],
        gate_output_gradient[None],
        both_input_gradients[None, rank:],
        up_output_gradient[None],
        (scale * dot(grad_lora, hidden, 0, 0)).astype(bf)[None],
        jnp.concatenate(down_grad, axis=1)[None],
    )


def solution(mesh):
    flat, deep = P(("ctx", "ep"), None), P(("ctx", "ep"), None, None)
    return jax.shard_map(
        local,
        mesh=mesh,
        in_specs=(flat,) * 4 + (deep,) * 11,
        out_specs=(flat,) + (deep,) * 6,
        check_vma=False,
    )
```
